32 devices in a mesh: dp: 8 (over y, x, core), tensor: 4 (over z).
Axes of the slice: x: 2, y: 2, z: 4, core: 2. Of those that a mesh axis runs over, the one named last changes fastest.
Arguments:
- tokens: bfloat16 [16384, 768], P('dp'), may hold values from -6 to 6
- timesteps: int32 [256], P('dp'), may hold values from 0 to 1999, as said below
- time_table: bfloat16 [2000, 768], P(None, 'tensor'), may hold values from -3 to 3
- w_qkv: bfloat16 [768, 3, 768], P(None, None, 'tensor'), may hold values from -0.21875 to 0.21875
- b_qv: float32 [2, 768], P(None, 'tensor'), may hold values from -2 to 2
- w_out: bfloat16 [768, 768], P('tensor'), may hold values from -0.625 to 0.625
- b_out: float32 [768], replicated, may hold values from -2 to 2
- w_in: bfloat16 [768, 3072], P(None, 'tensor'), may hold values from -0.21875 to 0.21875
- b_in: float32 [3072], P('tensor'), may hold values from -3 to 3
- w_back: bfloat16 [3072, 768], P('tensor'), may hold values from -0.109375 to 0.109375
- b_back: float32 [768], replicated, may hold values from -2 to 2
- gain_one: float32 [768], replicated, may hold values from 0.25 to 1.75
- shift_one: float32 [768], replicated, may hold values from -2 to 2
- gain_two: float32 [768], replicated, may hold values from 0.25 to 1.75
- shift_two: float32 [768], replicated, may hold values from -2 to 2
- cotangent: bfloat16 [16384, 768], P('dp'), may hold values from -6 to 6
Outputs:
- output: bfloat16 [16384, 768], P('dp')
- grad_tokens: bfloat16 [16384, 768], P('dp')
- grad_table: float32 [2000, 768], P(None, 'tensor')
- grad_wqkv: float32 [768, 3, 768], P('dp', None, 'tensor')
- grad_bqv: float32 [2, 768], P(None, 'tensor')
- grad_wout: float32 [768, 768], P('tensor', 'dp')
- grad_bout: float32 [768], replicated
- grad_win: float32 [768, 3072], P('dp', 'tensor')
- grad_bin: float32 [3072], P('tensor')
- grad_wback: float32 [3072, 768], P('tensor', 'dp')
- grad_bback: float32 [768], replicated
- grad_gain_one: float32 [768], replicated
- grad_shift_one: float32 [768], replicated
- grad_gain_two: float32 [768], replicated
- grad_shift_two: float32 [768], replicated
The draws below stay inside these ranges and needn't reach their ends.
Inputs may be any that keep to these rules, and one draw needn't show every extreme that they name: `timesteps`: diffusion step of each sentence, a row of time_table.
All inputs are finite; a program needn't handle non-finite values.
Results may differ from the reference program's by a relative error of at most 0.017.
Values may be sent and summed in bfloat16 or wider, within the bound.
No kernel may reach another device: no remote copies, remote signals or barrier semaphores. Data moves between devices by JAX's collectives and lax.ppermute only.
A program may use at most 192 MiB of HBM per device.

```python
import jax
import jax.numpy as jnp
from jax import lax

D = 768
HEAD = 64
FF = 3072
STEPS = 2000
LEN = 64
SENTS = 256
TOKENS = 16384
N_TENSOR = 4


def draw_timesteps(key, part):
    key = jax.random.fold_in(key, 7)
    first_key, second_key = jax.random.split(key)
    first_draw = jax.random.randint(first_key, (SENTS,), 0, STEPS)
    second_draw = jax.random.randint(second_key, (SENTS,), 0, STEPS)
    return jnp.minimum(first_draw, second_draw).astype(jnp.int32)


def raised(array, stream_key, source, target, shards_of, factor):
    def block_of(dim):
        return (jnp.arange(array.shape[dim]) // (array.shape[dim] // shards_of)).reshape((-1,) + (1,) * (array.ndim - 1 - dim))

    first = jax.random.permutation(stream_key, shards_of)[block_of(target)]
    far = (block_of(target) + shards_of // 2) % shards_of
    return jnp.where((block_of(source) == first) | (block_of(source) == far), factor * array, array)


def level_of(rng, shape, cuts, smallest, high):
    level = 1.0
    for dim, parts in cuts:
        heights = jax.random.uniform(jax.random.fold_in(jax.random.fold_in(rng, 6), dim), (parts,), jnp.float32, smallest / len(cuts), high / len(cuts))
        level = level * jnp.repeat(jnp.exp(heights), shape[dim] // parts).reshape((-1,) + (1,) * (len(shape) - 1 - dim))
    return level


def noise(stream_key, dims, deviation, reach, shards=(), kind=jnp.bfloat16):
    level = level_of(stream_key, dims, shards, -0.22, 0.18) if shards else 1.0
    entries = jax.random.normal(stream_key, dims, jnp.float32) * deviation * level
    return jnp.minimum(jnp.maximum(entries, -reach), reach).astype(kind)


def heavy_noise(key, shape, scale, limit, cuts, heavy, dtype=jnp.bfloat16):
    array = scale * jax.random.normal(key, shape, jnp.float32)
    if cuts:
        array = array * level_of(key, shape, cuts, -0.22, 0.18)
    return jnp.clip(raised(array, jax.random.fold_in(key, 3), *heavy), -limit, limit).astype(dtype)


def setup_inputs(seed: int = 0) -> dict:
    seeds = jax.random.split(jax.random.key(seed), 17)
    tokens = noise(seeds[0], (TOKENS, D), 1.0, 6.0, ((0, 8),))
    timesteps = draw_timesteps(jax.random.fold_in(seeds[16], 71), 0)
    time_table = noise(seeds[2], (STEPS, D), 0.5, 3.0, ((1, 4),))
    w_qkv = noise(seeds[3], (D, 3, D), D ** -0.5, 0.21875, ((2, 4),))
    b_qv = noise(seeds[4], (2, D), 0.3, 2.0, ((1, 4),), jnp.float32)
    w_out = noise(seeds[5], (D, D), (D // 8) ** -0.5, 0.625, ((0, 4),))
    b_out = noise(seeds[6], (D,), 0.3, 2.0, (), jnp.float32)
    w_in = noise(seeds[7], (D, FF), D ** -0.5, 0.21875, ((1, 4),))
    b_in = noise(seeds[8], (FF,), 0.5, 3.0, ((0, 4),), jnp.float32)
    w_back = noise(seeds[9], (FF, D), FF ** -0.5, 0.109375, ((0, 4),))
    b_back = noise(seeds[10], (D,), 0.3, 2.0, (), jnp.float32)
    gain_one = jnp.clip(1.0 + 0.15 * jax.random.normal(seeds[11], (D,), jnp.float32), 0.25, 1.75)
    shift_one = noise(seeds[12], (D,), 0.3, 2.0, (), jnp.float32)
    gain_two = jnp.clip(1.0 + 0.15 * jax.random.normal(seeds[13], (D,), jnp.float32), 0.25, 1.75)
    shift_two = noise(seeds[14], (D,), 0.3, 2.0, (), jnp.float32)
    cotangent = heavy_noise(seeds[15], (TOKENS, D), 1.0, 6.0, ((0, 8),), (0, 1, 8, 2.0))
    return {"tokens": tokens, "timesteps": timesteps, "time_table": time_table, "w_qkv": w_qkv, "b_qv": b_qv, "w_out": w_out, "b_out": b_out, "w_in": w_in, "b_in": b_in, "w_back": w_back, "b_back": b_back, "gain_one": gain_one, "shift_one": shift_one, "gain_two": gain_two, "shift_two": shift_two, "cotangent": cotangent}


EPS = 1e-05
HIGHEST_PREC = lax.Precision.HIGHEST

@jax.custom_vjp
def low(v):
    return lax.optimization_barrier(v.astype(jnp.bfloat16)).astype(jnp.float32)

@jax.custom_vjp
def low_back(v):
    return v

def low_keep(v):
    return (low(v), None)

def low_pass(kept, grad):
    return (grad,)

def back_keep(v):
    return (v, None)

def back_low(kept, grad):
    return (low(grad),)
low.defvjp(low_keep, low_pass)
low_back.defvjp(back_keep, back_low)

def matmul_high(left, right):
    return jnp.dot(left, right, precision=HIGHEST_PREC)

def norm_rows(rows, gain, shift):
    mean = lax.optimization_barrier(jnp.mean(rows, axis=-1, keepdims=True))
    centred = rows - mean
    spread = lax.optimization_barrier(jnp.mean(centred * centred, axis=-1, keepdims=True))
    return centred * lax.rsqrt(spread + EPS) * gain + shift

def layer(block_tokens, block_time, params):
    w_qkv, b_qv, w_out, b_out, w_in, b_in, w_back, b_back, gain_one, shift_one, gain_two, shift_two = params
    sent_count = block_tokens.shape[0]
    entry_rows = (block_tokens + block_time[:, None, :]).reshape(sent_count * LEN, D)
    n_one = low(norm_rows(entry_rows, gain_one, shift_one))
    head_cols = D // N_TENSOR
    hidden_dev = FF // N_TENSOR
    attended = jnp.zeros_like(entry_rows)
    for shard in range(N_TENSOR):
        columns = slice(shard * head_cols, (shard + 1) * head_cols)
        queries = low(low_back(matmul_high(n_one, w_qkv[:, 0, columns]) + b_qv[0, columns]))
        key_heads = low(low_back(matmul_high(n_one, w_qkv[:, 1, columns])))
        values = low(low_back(matmul_high(n_one, w_qkv[:, 2, columns]) + b_qv[1, columns]))
        queries = queries.reshape(sent_count, LEN, -1, HEAD)
        key_heads = key_heads.reshape(sent_count, LEN, -1, HEAD)
        values = values.reshape(sent_count, LEN, -1, HEAD)
        scores = low_back(jnp.einsum('nqhe,nkhe->nhqk', queries, key_heads, precision=HIGHEST_PREC) * HEAD ** (-0.5))
        prob_low = low(jax.nn.softmax(scores, axis=-1))
        mixed_heads = jnp.einsum('nhqk,nkhe->nqhe', prob_low, values, precision=HIGHEST_PREC)
        mixed_heads = low(low_back(mixed_heads.reshape(sent_count * LEN, head_cols)))
        attended = attended + low(low_back(matmul_high(mixed_heads, w_out[columns])))
    middle = entry_rows + attended + b_out
    n_two = low(norm_rows(middle, gain_two, shift_two))
    summed = jnp.zeros_like(middle)
    for shard in range(N_TENSOR):
        units = slice(shard * hidden_dev, (shard + 1) * hidden_dev)
        pre_act = low_back(matmul_high(n_two, w_in[:, units]) + b_in[units])
        activated = low(jax.nn.gelu(pre_act, approximate=False))
        summed = summed + low(matmul_high(activated, w_back[units]))
    return (middle + summed + b_back).reshape(sent_count, LEN, D)

def reference(tokens, timesteps, time_table, w_qkv, b_qv, w_out, b_out, w_in, b_in, w_back, b_back, gain_one, shift_one, gain_two, shift_two, cotangent):
    group_size = min(max(4096 // LEN, 1), SENTS)
    blocks = SENTS // group_size
    table_f32 = time_table.astype(jnp.float32)
    params = tuple((p.astype(jnp.float32) for p in (w_qkv, b_qv, w_out, b_out, w_in, b_in, w_back, b_back, gain_one, shift_one, gain_two, shift_two)))
    token_blocks = tokens.astype(jnp.float32).reshape(blocks, group_size, LEN, D)
    cot_blocks = cotangent.astype(jnp.float32).reshape(blocks, group_size, LEN, D)
    step_blocks = timesteps.reshape(blocks, group_size)

    def one_block(carry, pieces):
        grad_sums, table_grad = carry
        block_tokens, block_cot, block_steps = pieces
        block_time = table_f32[block_steps]
        result, pull_back = jax.vjp(layer, block_tokens, block_time, params)
        grad_block, grad_time, grad_params = pull_back(block_cot)
        grad_sums = jax.tree.map(jnp.add, grad_sums, grad_params)
        table_grad = table_grad.at[block_steps].add(grad_time)
        return ((grad_sums, table_grad), (result.astype(jnp.bfloat16), grad_block.astype(jnp.bfloat16)))
    zeros = jax.tree.map(jnp.zeros_like, params)
    (grad_sums, table_grad), (outputs, grad_rows) = lax.scan(one_block, (zeros, jnp.zeros_like(table_f32)), (token_blocks, cot_blocks, step_blocks))
    return (outputs.reshape(TOKENS, D), grad_rows.reshape(TOKENS, D), table_grad, grad_sums[0], grad_sums[1], grad_sums[2], grad_sums[3], grad_sums[4], grad_sums[5], grad_sums[6], grad_sums[7], grad_sums[8], grad_sums[9], grad_sums[10], grad_sums[11])
```

```python
import functools

import jax
import jax.numpy as jnp
from jax import lax
from jax.experimental import pallas as pl
from jax.experimental.pallas import tpu as pltpu
from jax.sharding import PartitionSpec as P

HEAD = 64
LEN = 64
EPS = 1e-05
BR = 256
VMEM_BYTES = 56 * 1024 * 1024
HIGHEST_PREC = lax.Precision.HIGHEST
F32 = jnp.float32
BF16 = jnp.bfloat16


def dot_nn(a, b):
    return lax.dot_general(a, b, (((1,), (0,)), ((), ())), preferred_element_type=F32)


def dot_nt(a, b):
    return lax.dot_general(a, b, (((1,), (1,)), ((), ())), preferred_element_type=F32)


def dot_tn(a, b):
    return lax.dot_general(a, b, (((0,), (0,)), ((), ())), preferred_element_type=F32)


def params():
    return pltpu.CompilerParams(
        dimension_semantics=("arbitrary",), vmem_limit_bytes=VMEM_BYTES
    )


def rows_spec(width, rows=BR):
    return pl.BlockSpec((rows, width), lambda i, *_: (i, 0))


def whole_spec(shape):
    return pl.BlockSpec(shape, lambda i, *_: (0,) * len(shape))


def slot_spec(shape, k):
    return pl.BlockSpec((1,) + shape, lambda i, s: (s[k],) + (0,) * len(shape))


def normed(x):
    mean = jnp.mean(x, axis=-1, keepdims=True)
    centred = x - mean
    spread = jnp.mean(centred * centred, axis=-1, keepdims=True)
    inv = lax.rsqrt(spread + EPS)
    return centred * inv, inv


def norm_back(d_out, gain, xhat, inv):
    gy = d_out * gain
    m1 = jnp.mean(gy, axis=-1, keepdims=True)
    m2 = jnp.mean(gy * xhat, axis=-1, keepdims=True)
    return inv * (gy - m1 - xhat * m2)


def fold8(x):
    return jnp.sum(x.reshape(x.shape[0] // 8, 8, x.shape[1]), axis=0)


def entry_of(tok_ref, time_ref):
    tok = tok_ref[...].astype(F32)
    n = tok.shape[0] // LEN
    return (tok.reshape(n, LEN, tok.shape[1]) + time_ref[0][:, None, :]).reshape(tok.shape)


def half_masks():
    lane = lax.broadcasted_iota(jnp.int32, (LEN, 2 * HEAD), 1)
    low = (lane < HEAD).astype(F32)
    return low.astype(BF16), (1.0 - low).astype(BF16), lane < HEAD


def block_diag(x, mlo, mhi):
    return jnp.concatenate([x * mlo, x * mhi], axis=0)


def load_pair(wa_ref, wb_ref, wqkv, wo):
    hc = HEAD * 3
    for t in range(3):
        wqkv[2 * t * hc : (2 * t + 1) * hc, :] = wa_ref[0, t * hc : (t + 1) * hc, :]
        wqkv[(2 * t + 1) * hc : (2 * t + 2) * hc, :] = wb_ref[0, t * hc : (t + 1) * hc, :]
    wo[:hc, :] = wa_ref[0, 3 * hc :, :]
    wo[hc:, :] = wb_ref[0, 3 * hc :, :]


def attend(n_one, wqkv, wo, bias, qkv_ref, p_ref, mix_ref):
    width = wo.shape[0]
    qkv_ref[...] = (dot_nt(n_one, wqkv[...]) + bias).astype(BF16)
    mlo, mhi, low = half_masks()
    for s in range(n_one.shape[0] // LEN):
        rows = slice(s * LEN, (s + 1) * LEN)
        for j in range(width // 128):
            cols = slice(j * 128, (j + 1) * 128)
            q = qkv_ref[rows, j * 128 : (j + 1) * 128]
            k = qkv_ref[rows, width + j * 128 : width + (j + 1) * 128]
            v = qkv_ref[rows, 2 * width + j * 128 : 2 * width + (j + 1) * 128]
            scores = dot_nt(k, block_diag(q, mlo, mhi))
            top = jnp.max(scores, axis=0, keepdims=True)
            e = jnp.exp((scores - top) * (HEAD**-0.5))
            p = (e * (1.0 / jnp.sum(e, axis=0, keepdims=True))).astype(BF16)
            p_ref[rows, cols] = p
            r = dot_tn(p, v)
            mix_ref[rows, cols] = jnp.where(low, r[:LEN], r[LEN:]).astype(BF16)
    return dot_nn(mix_ref[...], wo[...])


def attend_first(
    slots, tok, time, g1, s1, wa, wb, bias, n_one_ref, qkv_ref, p_ref, mix_ref, part_ref, wqkv, wo
):
    @pl.when(pl.program_id(0) == 0)
    def _():
        load_pair(wa, wb, wqkv, wo)

    xhat, _ = normed(entry_of(tok, time))
    n_one = (xhat * g1[...] + s1[...]).astype(BF16)
    n_one_ref[...] = n_one
    part_ref[...] = attend(n_one, wqkv, wo, bias[...], qkv_ref, p_ref, mix_ref)


def attend_last(
    slots, tok, time, n_one, part, bout, g2, s2, wa, wb, bias,
    qkv_ref, p_ref, middle_ref, n_two_ref, wqkv, wo, mix_ref,
):
    @pl.when(pl.program_id(0) == 0)
    def _():
        load_pair(wa, wb, wqkv, wo)

    more = attend(n_one[...], wqkv, wo, bias[...], qkv_ref, p_ref, mix_ref)
    middle = entry_of(tok, time) + part[...] + more + bout[...]
    middle_ref[...] = middle
    xhat, _ = normed(middle)
    n_two_ref[...] = (xhat * g2[...] + s2[...]).astype(BF16)


ERF_P = 0.3275911
ERF_A = (0.254829592, -0.284496736, 1.421413741, -1.453152027, 1.061405429)


def gelu_both(x):
    bell = jnp.exp(x * x * (-0.5))
    t = 1.0 / (1.0 + jnp.abs(x) * (ERF_P * 0.5**0.5))
    poly = t * (
        0.5 * ERF_A[0]
        + t * (0.5 * ERF_A[1] + t * (0.5 * ERF_A[2] + t * (0.5 * ERF_A[3] + t * (0.5 * ERF_A[4]))))
    )
    tail = poly * bell
    cdf = jnp.where(x >= 0, 1.0 - tail, tail)
    return x * cdf, cdf + x * bell * 0.3989422804014327


def mlp_slot(n_two, c, wi, wb, b):
    pre = dot_nt(n_two, wi) + b
    d_act = dot_nt(c, wb)
    act, slope = gelu_both(pre)
    act = act.astype(BF16)
    d_pre = (d_act * slope).astype(BF16)
    return act, d_pre


def mlp_first(n_two, c, wi, wb, b, out_ref, dn2_ref, act_ref, dpre_ref, gbin_ref):
    act, d_pre = mlp_slot(n_two[...], c[...], wi[...], wb[...], b[...])
    act_ref[...] = act
    dpre_ref[...] = d_pre

    @pl.when(pl.program_id(0) == 0)
    def _():
        gbin_ref[...] = jnp.zeros_like(gbin_ref)

    gbin_ref[...] += fold8(d_pre.astype(F32))
    out_ref[...] = dot_nn(act, wb[...])
    dn2_ref[...] = dot_nn(d_pre, wi[...])


def mlp_rest(
    slots, n_two, c, middle, out_in, dn2_in, g2, bback, w1, w2, w3, b,
    out_ref, dmid_ref, dml_ref, sums_ref,
):
    hid = b.shape[-1] // 3
    out = out_in[...]
    dn2 = dn2_in[...]
    for k, w in enumerate((w1, w2, w3)):
        wi = w[0, :hid, :]
        wb = w[0, hid:, :]
        act, d_pre = mlp_slot(n_two[...], c[...], wi, wb, b[:, k * hid : (k + 1) * hid])
        out = out + dot_nn(act, wb)
        dn2 = dn2 + dot_nn(d_pre, wi)
    mid = middle[...]
    cot = c[...].astype(F32)
    out_ref[...] = (mid + out + bback[...]).astype(BF16)
    xhat, inv = normed(mid)
    d_mid = cot + norm_back(dn2, g2[...], xhat, inv)
    dmid_ref[...] = d_mid
    dml_ref[...] = d_mid.astype(BF16)

    @pl.when(pl.program_id(0) == 0)
    def _():
        sums_ref[...] = jnp.zeros_like(sums_ref)

    sums_ref[0:8, :] += fold8(dn2 * xhat)
    sums_ref[8:16, :] += fold8(dn2)
    sums_ref[16:24, :] += fold8(d_mid)
    sums_ref[24:32, :] += fold8(cot)


def attend_back(dml, qkv, p, wqkv, wo, dqkv, dmix):
    width = wo.shape[0]
    scale = HEAD**-0.5
    dmix[...] = dot_nt(dml, wo[...]).astype(BF16)
    mlo, mhi, low = half_masks()
    for s in range(dml.shape[0] // LEN):
        rows = slice(s * LEN, (s + 1) * LEN)
        for j in range(width // 128):
            cols = slice(j * 128, (j + 1) * 128)
            kcols = slice(width + j * 128, width + (j + 1) * 128)
            vcols = slice(2 * width + j * 128, 2 * width + (j + 1) * 128)
            q, k, v = qkv[rows, cols], qkv[rows, kcols], qkv[rows, vcols]
            prob = p[rows, cols]
            d_out = block_diag(dmix[rows, cols], mlo, mhi)
            dqkv[rows, vcols] = dot_nn(prob, d_out).astype(BF16)
            d_p = dot_nt(v, d_out)
            pf = prob.astype(F32)
            dot = jnp.sum(pf * d_p, axis=0, keepdims=True)
            d_s = (pf * (d_p - dot)).astype(BF16)
            dqkv[rows, kcols] = (dot_nn(d_s, block_diag(q, mlo, mhi)) * scale).astype(BF16)
            r = dot_tn(d_s, k)
            dqkv[rows, cols] = (jnp.where(low, r[:LEN], r[LEN:]) * scale).astype(BF16)
    return dot_nn(dqkv[...], wqkv[...])


def back_first(slots, dml, qkv, p, wa, wb, dn1_ref, dq_ref, dk_ref, dv_ref, sums_ref, wqkv, wo, dqkv, dmix):
    @pl.when(pl.program_id(0) == 0)
    def _():
        load_pair(wa, wb, wqkv, wo)
        sums_ref[...] = jnp.zeros_like(sums_ref)

    dn1_ref[...] = attend_back(dml[...], qkv, p, wqkv, wo, dqkv, dmix)
    hc = HEAD * 3
    width = 2 * hc
    for t, ref in enumerate((dq_ref, dk_ref, dv_ref)):
        ref[...] = dqkv[:, t * width : t * width + hc]
    sums_ref[...] += fold8(dqkv[...].astype(F32))


def back_last(
    slots, tok, time, dml, dmid, dn1, g1, qkv, p, wa, wb,
    gtok_ref, sent_ref, sums_ref, wqkv, wo, dqkv, dmix,
):
    @pl.when(pl.program_id(0) == 0)
    def _():
        load_pair(wa, wb, wqkv, wo)
        sums_ref[...] = jnp.zeros_like(sums_ref)

    d_n = dn1[...] + attend_back(dml[...], qkv, p, wqkv, wo, dqkv, dmix)
    xhat, inv = normed(entry_of(tok, time))
    d_entry = dmid[...] + norm_back(d_n, g1[...], xhat, inv)
    gtok_ref[...] = d_entry.astype(BF16)
    sent_ref[0] = jnp.sum(d_entry.reshape(d_entry.shape[0] // LEN, LEN, -1), axis=1)
    sums_ref[0:8, :] += fold8(d_n * xhat)
    sums_ref[8:16, :] += fold8(d_n)


def call(kernel, grid, in_specs, out_specs, out_shape, scratch, slots, args):
    if slots is None:
        return pl.pallas_call(
            kernel, grid=grid, in_specs=in_specs, out_specs=out_specs, out_shape=out_shape,
            scratch_shapes=scratch, compiler_params=params(),
        )(*args)
    return pl.pallas_call(
        kernel,
        grid_spec=pltpu.PrefetchScalarGridSpec(
            num_scalar_prefetch=1, grid=grid, in_specs=in_specs, out_specs=out_specs,
            scratch_shapes=scratch,
        ),
        out_shape=out_shape,
        compiler_params=params(),
    )(slots, *args)


def body(
    tokens, timesteps, time_table, w_qkv, b_qv, w_out, b_out, w_in, b_in, w_back, b_back,
    gain_one, shift_one, gain_two, shift_two, cotangent,
):
    sentences = timesteps.shape[0]
    rows, dim = tokens.shape
    hc = w_out.shape[0]
    hid = w_back.shape[0]
    table_cols = time_table.shape[1]
    n_tensor = dim // hc
    me = lax.axis_index("tensor")
    part = lax.axis_index("dp")
    dp = lax.axis_size("dp")
    slots = (me ^ jnp.arange(n_tensor, dtype=jnp.int32)).astype(jnp.int32)

    steps_iota = lax.broadcasted_iota(jnp.int32, (sentences, time_table.shape[0]), 1)
    picked = timesteps[:, None] == steps_iota
    own_rows = jnp.dot(picked.astype(BF16), time_table, preferred_element_type=F32).astype(BF16)
    time_rows = lax.all_gather(own_rows, "tensor", axis=1, tiled=True).astype(F32)
    time_blocks = time_rows.reshape(rows // BR, BR // LEN, dim)

    att_own = jnp.concatenate(
        [jnp.transpose(w_qkv, (1, 2, 0)).reshape(3 * hc, dim), w_out], axis=0
    )
    wi_own = w_in.T
    mlp_own = jnp.concatenate([wi_own, w_back], axis=0)

    def everywhere(shard):
        n = shard.shape[0] // dp
        piece = lax.dynamic_slice_in_dim(shard, part * n, n, 0)
        return lax.all_gather(piece, ("tensor", "dp"), axis=0, tiled=True).reshape(
            n_tensor, shard.shape[0], dim
        )

    att_all = everywhere(att_own)
    mlp_all = everywhere(mlp_own)
    biases = lax.all_gather(jnp.concatenate([b_qv.reshape(-1), b_in]), "tensor", axis=0)
    biases = jnp.take(biases, slots, axis=0)
    bq, bv, bi = biases[:, :hc], biases[:, hc : 2 * hc], biases[:, 2 * hc :]
    no_bias = jnp.zeros((2 * hc,), F32)

    def pair_bias(k):
        return jnp.concatenate(
            [bq[k : k + 2].reshape(-1), no_bias, bv[k : k + 2].reshape(-1)]
        ).reshape(1, 6 * hc)

    row = lambda v: v.reshape(1, -1)
    nb = rows // BR
    grid = (nb,)
    time_spec = pl.BlockSpec((1, BR // LEN, dim), lambda i, *_: (i, 0, 0))
    vec = whole_spec((1, dim))
    att_spec = lambda k: slot_spec((4 * hc, dim), k)
    pair_scr = [pltpu.VMEM((6 * hc, dim), BF16), pltpu.VMEM((2 * hc, dim), BF16)]
    sds = jax.ShapeDtypeStruct

    n_one, qkv_a, p_a, mix_a, attn_part = call(
        attend_first, grid,
        [rows_spec(dim), time_spec, vec, vec, att_spec(0), att_spec(1), whole_spec((1, 6 * hc))],
        [rows_spec(dim), rows_spec(6 * hc), rows_spec(2 * hc), rows_spec(2 * hc), rows_spec(dim)],
        [sds((rows, dim), BF16), sds((rows, 6 * hc), BF16), sds((rows, 2 * hc), BF16),
         sds((rows, 2 * hc), BF16), sds((rows, dim), F32)],
        pair_scr, slots,
        (tokens, time_blocks, row(gain_one), row(shift_one), att_all, att_all, pair_bias(0)),
    )
    qkv_b, p_b, middle, n_two = call(
        attend_last, grid,
        [rows_spec(dim), time_spec, rows_spec(dim), rows_spec(dim), vec, vec, vec,
         att_spec(2), att_spec(3), whole_spec((1, 6 * hc))],
        [rows_spec(6 * hc), rows_spec(2 * hc), rows_spec(dim), rows_spec(dim)],
        [sds((rows, 6 * hc), BF16), sds((rows, 2 * hc), BF16), sds((rows, dim), F32),
         sds((rows, dim), BF16)],
        pair_scr + [pltpu.VMEM((BR, 2 * hc), BF16)], slots,
        (tokens, time_blocks, n_one, attn_part, row(b_out), row(gain_two), row(shift_two),
         att_all, att_all, pair_bias(2)),
    )
    out_acc, dn2_acc, act, d_pre, gbin = call(
        mlp_first, grid,
        [rows_spec(dim), rows_spec(dim), whole_spec((hid, dim)), whole_spec((hid, dim)),
         whole_spec((1, hid))],
        [rows_spec(dim), rows_spec(dim), rows_spec(hid), rows_spec(hid), whole_spec((8, hid))],
        [sds((rows, dim), F32), sds((rows, dim), F32), sds((rows, hid), BF16),
         sds((rows, hid), BF16), sds((8, hid), F32)],
        [], None,
        (n_two, cotangent, wi_own, w_back, row(b_in)),
    )
    mlp_spec = lambda k: slot_spec((2 * hid, dim), k)
    output, d_mid, d_mid_low, sums_two = call(
        mlp_rest, grid,
        [rows_spec(dim), rows_spec(dim), rows_spec(dim), rows_spec(dim), rows_spec(dim), vec, vec,
         mlp_spec(1), mlp_spec(2), mlp_spec(3), whole_spec((1, 3 * hid))],
        [rows_spec(dim), rows_spec(dim), rows_spec(dim), whole_spec((32, dim))],
        [sds((rows, dim), BF16), sds((rows, dim), F32), sds((rows, dim), BF16),
         sds((32, dim), F32)],
        [], slots,
        (n_two, cotangent, middle, out_acc, dn2_acc, row(gain_two), row(b_back),
         mlp_all, mlp_all, mlp_all, bi[1:].reshape(1, -1)),
    )
    back_scr = pair_scr + [pltpu.VMEM((BR, 6 * hc), BF16), pltpu.VMEM((BR, 2 * hc), BF16)]
    dn1_acc, d_q, d_k, d_v, sums_qkv = call(
        back_first, grid,
        [rows_spec(dim), rows_spec(6 * hc), rows_spec(2 * hc), att_spec(0), att_spec(1)],
        [rows_spec(dim), rows_spec(hc), rows_spec(hc), rows_spec(hc), whole_spec((8, 6 * hc))],
        [sds((rows, dim), F32)] + [sds((rows, hc), BF16)] * 3 + [sds((8, 6 * hc), F32)],
        back_scr, slots,
        (d_mid_low, qkv_a, p_a, att_all, att_all),
    )
    grad_tokens, per_sentence, sums_one = call(
        back_last, grid,
        [rows_spec(dim), time_spec, rows_spec(dim), rows_spec(dim), rows_spec(dim), vec,
         rows_spec(6 * hc), rows_spec(2 * hc), att_spec(2), att_spec(3)],
        [rows_spec(dim), time_spec, whole_spec((16, dim))],
        [sds((rows, dim), BF16), sds((nb, BR // LEN, dim), F32), sds((16, dim), F32)],
        back_scr, slots,
        (tokens, time_blocks, d_mid_low, d_mid, dn1_acc, row(gain_one), qkv_b, p_b,
         att_all, att_all),
    )

    def scattered(grad):
        return lax.psum_scatter(
            grad.astype(BF16), "dp", scatter_dimension=0, tiled=True
        ).astype(F32)

    grad_win = scattered(dot_tn(n_two, d_pre))
    grad_wback = scattered(dot_tn(cotangent, act)).T
    grad_wout = scattered(dot_tn(d_mid_low, mix_a[:, :hc])).T
    grad_wqkv = scattered(
        jnp.stack([dot_tn(n_one, d) for d in (d_q, d_k, d_v)], axis=1)
    )

    own_cols = lax.dynamic_slice_in_dim(
        per_sentence.reshape(sentences, dim), me * table_cols, table_cols, 1
    )
    all_cols = lax.all_gather(own_cols, "dp", axis=0, tiled=True)
    all_steps = lax.all_gather(timesteps, "dp", axis=0, tiled=True)
    all_picked = all_steps[:, None] == lax.broadcasted_iota(
        jnp.int32, (all_steps.shape[0], time_table.shape[0]), 1
    )
    grad_table = lax.dot_general(
        all_picked.astype(F32), all_cols, (((0,), (0,)), ((), ())),
        precision=HIGHEST_PREC, preferred_element_type=F32,
    )
    sums_two = jnp.sum(sums_two.reshape(4, 8, dim), axis=1)
    sums_one = jnp.sum(sums_one.reshape(2, 8, dim), axis=1)
    sums_qkv = jnp.sum(sums_qkv, axis=0)
    small = lax.psum(
        jnp.concatenate(
            [sums_two.reshape(-1), sums_one.reshape(-1), jnp.sum(gbin, axis=0),
             sums_qkv[:hc], sums_qkv[4 * hc : 5 * hc]]
        ),
        "dp",
    )
    cut = lambda k: small[k * dim : (k + 1) * dim]
    base = 6 * dim
    grad_bin = small[base : base + hid]
    grad_bqv = small[base + hid :].reshape(2, hc)
    return (
        output, grad_tokens, grad_table, grad_wqkv, grad_bqv, grad_wout, cut(2), grad_win,
        grad_bin, grad_wback, cut(3), cut(4), cut(5), cut(0), cut(1),
    )


def solution(mesh):
    return jax.shard_map(
        body,
        mesh=mesh,
        in_specs=(
            P("dp", None), P("dp"), P(None, "tensor"), P(None, None, "tensor"), P(None, "tensor"),
            P("tensor", None), P(), P(None, "tensor"), P("tensor"), P("tensor", None), P(), P(),
            P(), P(), P(), P("dp", None),
        ),
        out_specs=(
            P("dp", None), P("dp", None), P(None, "tensor"), P("dp", None, "tensor"),
            P(None, "tensor"), P("tensor", "dp"), P(), P("dp", "tensor"), P("tensor"),
            P("tensor", "dp"), P(), P(), P(), P(), P(),
        ),
        check_vma=False,
    )
```

```python
import functools

import jax
import jax.numpy as jnp
from jax import lax
from jax.experimental import pallas as pl
from jax.experimental.pallas import tpu as pltpu
from jax.sharding import PartitionSpec as P

HEAD = 64
HEADS = 3
LEN = 64
EPS = 1e-05
BR = 512
VMEM_BYTES = 58 * 1024 * 1024
HIGHEST_PREC = lax.Precision.HIGHEST
F32 = jnp.float32
BF16 = jnp.bfloat16


def dot_nn(a, b):
    return lax.dot_general(a, b, (((1,), (0,)), ((), ())), preferred_element_type=F32)


def dot_nt(a, b):
    return lax.dot_general(a, b, (((1,), (1,)), ((), ())), preferred_element_type=F32)


def dot_tn(a, b):
    return lax.dot_general(a, b, (((0,), (0,)), ((), ())), preferred_element_type=F32)


def params():
    return pltpu.CompilerParams(
        dimension_semantics=("arbitrary",), vmem_limit_bytes=VMEM_BYTES
    )


def rows_spec(width, rows=BR):
    return pl.BlockSpec((rows, width), lambda i, *_: (i, 0))


def whole_spec(shape):
    return pl.BlockSpec(shape, lambda i, *_: (0,) * len(shape))


def slot_spec(shape, k):
    return pl.BlockSpec((1,) + shape, lambda i, s: (s[k],) + (0,) * len(shape))


def normed(x):
    mean = jnp.mean(x, axis=-1, keepdims=True)
    centred = x - mean
    spread = jnp.mean(centred * centred, axis=-1, keepdims=True)
    inv = lax.rsqrt(spread + EPS)
    return centred * inv, inv


def norm_back(d_out, gain, xhat, inv):
    gy = d_out * gain
    m1 = jnp.mean(gy, axis=-1, keepdims=True)
    m2 = jnp.mean(gy * xhat, axis=-1, keepdims=True)
    return inv * (gy - m1 - xhat * m2)


def fold8(x):
    return jnp.sum(x.reshape(x.shape[0] // 8, 8, x.shape[1]), axis=0)


def entry_of(tok_ref, time_ref):
    tok = tok_ref[...].astype(F32)
    n = tok.shape[0] // LEN
    return (tok.reshape(n, LEN, tok.shape[1]) + time_ref[...][:, None, :]).reshape(tok.shape)


def half_masks():
    lane = lax.broadcasted_iota(jnp.int32, (LEN, 2 * HEAD), 1)
    low = (lane < HEAD).astype(F32)
    return low.astype(BF16), (1.0 - low).astype(BF16), lane < HEAD


def block_diag(x, mlo, mhi):
    return jnp.concatenate([x * mlo, x * mhi], axis=0)


def load_own(att, wqkv, wo):
    hc = HEADS * HEAD
    width = wo.shape[0]
    wqkv[...] = jnp.zeros_like(wqkv)
    wo[...] = jnp.zeros_like(wo)
    for t in range(3):
        wqkv[t * width : t * width + hc, :] = att[t * hc : (t + 1) * hc, :]
    wo[:hc, :] = att[3 * hc :, :]


def load_rest(core, mine, other, wqkv, wo):
    hc = HEADS * HEAD
    n = hc // 2
    width = wo.shape[0]
    wqkv[...] = jnp.zeros_like(wqkv)
    wo[...] = jnp.zeros_like(wo)
    for s in range(3):
        for src, at in ((mine, core * n), (other, (1 - core) * n)):
            for t in range(3):
                wqkv[pl.ds(pl.multiple_of(t * width + s * hc + at, 16), n), :] = src[t, s]
            wo[pl.ds(pl.multiple_of(s * hc + at, 16), n), :] = src[3, s]


def tile_list(rows, width):
    return [(s, j) for s in range(rows // LEN) for j in range(width // 128)]


def tile(ref, st, part=0, width=0):
    s, j = st
    return ref[s * LEN : (s + 1) * LEN, part * width + j * 128 : part * width + (j + 1) * 128]


def put_tile(ref, st, value, part=0, width=0):
    s, j = st
    ref[s * LEN : (s + 1) * LEN, part * width + j * 128 : part * width + (j + 1) * 128] = (
        value.astype(BF16)
    )


def attend(n_one, wqkv, wo, bias, qkv_ref, p_ref, mix_ref):
    width = wo.shape[0]
    qkv_ref[...] = (dot_nt(n_one, wqkv[...]) + bias).astype(BF16)
    mlo, mhi, low = half_masks()
    tiles = tile_list(n_one.shape[0], width)
    scores = [
        dot_nt(tile(qkv_ref, t, 1, width), block_diag(tile(qkv_ref, t, 0, width), mlo, mhi))
        for t in tiles
    ]
    probs = []
    for t, sc in zip(tiles, scores):
        top = jnp.max(sc, axis=0, keepdims=True)
        e = jnp.exp((sc - top) * (HEAD**-0.5))
        p = (e * (1.0 / jnp.sum(e, axis=0, keepdims=True))).astype(BF16)
        probs.append(p)
        put_tile(p_ref, t, p)
    both = [dot_tn(p, tile(qkv_ref, t, 2, width)) for t, p in zip(tiles, probs)]
    for t, r in zip(tiles, both):
        put_tile(mix_ref, t, jnp.where(low, r[:LEN], r[LEN:]))
    return dot_nn(mix_ref[...], wo[...])


def attend_own(
    tok, time, vecs, own, n_one_ref, qkv_ref, p_ref, mix_ref, part_ref, wqkv, wo,
):
    @pl.when(pl.program_id(0) == 0)
    def _():
        load_own(own, wqkv, wo)

    xhat, _ = normed(entry_of(tok, time))
    n_one = (xhat * vecs[0:1, :] + vecs[1:2, :]).astype(BF16)
    n_one_ref[...] = n_one
    part_ref[...] = attend(n_one, wqkv, wo, vecs[7:8, :], qkv_ref, p_ref, mix_ref)


def attend_rest(
    core, tok, time, n_one, part, vecs, mine, other, bias,
    qkv_ref, p_ref, middle_ref, n_two_ref, wqkv, wo, mix_ref,
):
    @pl.when(pl.program_id(0) == 0)
    def _():
        load_rest(core[0], mine, other, wqkv, wo)

    more = attend(n_one[...], wqkv, wo, bias[...], qkv_ref, p_ref, mix_ref)
    middle = entry_of(tok, time) + part[...] + more + vecs[4:5, :]
    middle_ref[...] = middle
    xhat, _ = normed(middle)
    n_two_ref[...] = (xhat * vecs[2:3, :] + vecs[3:4, :]).astype(BF16)


ERF_P = 0.3275911
ERF_A = (0.254829592, -0.284496736, 1.421413741, -1.453152027, 1.061405429)


def gelu_both(x):
    bell = jnp.exp(x * x * (-0.5))
    t = 1.0 / (1.0 + jnp.abs(x) * (ERF_P * 0.5**0.5))
    poly = t * (
        0.5 * ERF_A[0]
        + t * (0.5 * ERF_A[1] + t * (0.5 * ERF_A[2] + t * (0.5 * ERF_A[3] + t * (0.5 * ERF_A[4]))))
    )
    tail = poly * bell
    cdf = jnp.where(x >= 0, 1.0 - tail, tail)
    return x * cdf, cdf + x * bell * 0.3989422804014327


def mlp_slot(n_two, c, wi, wb, b):
    pre = dot_nt(n_two, wi) + b
    d_act = dot_nt(c, wb)
    act, slope = gelu_both(pre)
    act = act.astype(BF16)
    d_pre = (d_act * slope).astype(BF16)
    return act, d_pre


def mlp_own(n_two, c, wi, wb, vecs, out_ref, dn2_ref, grad_ref, gbin_ref, acc, sums):
    hid = wi.shape[0]

    @pl.when(pl.program_id(0) == 0)
    def _():
        acc[...] = jnp.zeros_like(acc)
        sums[...] = jnp.zeros_like(sums)

    act, d_pre = mlp_slot(n_two[...], c[...], wi[...], wb[...], vecs[6:7, :])
    sums[...] += fold8(d_pre.astype(F32))
    out_ref[...] = dot_nn(act, wb[...])
    dn2_ref[...] = dot_nn(d_pre, wi[...])
    acc[:, :hid] += dot_tn(n_two[...], d_pre)
    acc[:, hid:] += dot_tn(c[...], act)

    @pl.when(pl.program_id(0) == pl.num_programs(0) - 1)
    def _():
        grad_ref[...] = acc[...].astype(BF16)
        gbin_ref[...] = jnp.sum(sums[...], axis=0, keepdims=True)


def mlp_rest(
    slots, n_two, c, middle, out_in, dn2_in, vecs, w1, w2, w3, b,
    out_ref, dmid_ref, dml_ref, sums_ref, sums,
):
    hid = b.shape[-1]
    out = out_in[...]
    dn2 = dn2_in[...]
    for k, w in enumerate((w1, w2, w3)):
        wi = w[0, :hid, :]
        wb = w[0, hid:, :]
        act, d_pre = mlp_slot(n_two[...], c[...], wi, wb, b[k : k + 1, :])
        out = out + dot_nn(act, wb)
        dn2 = dn2 + dot_nn(d_pre, wi)
    mid = middle[...]
    cot = c[...].astype(F32)
    out_ref[...] = (mid + out + vecs[5:6, :]).astype(BF16)
    xhat, inv = normed(mid)
    d_mid = cot + norm_back(dn2, vecs[2:3, :], xhat, inv)
    dmid_ref[...] = d_mid
    dml_ref[...] = d_mid.astype(BF16)
    add_sums(sums, sums_ref, (dn2 * xhat, dn2, d_mid, cot))


def add_sums(sums, sums_ref, terms):
    @pl.when(pl.program_id(0) == 0)
    def _():
        sums[...] = jnp.zeros_like(sums)

    for k, term in enumerate(terms):
        sums[8 * k : 8 * k + 8, :] += fold8(term)

    @pl.when(pl.program_id(0) == pl.num_programs(0) - 1)
    def _():
        for k in range(len(terms)):
            sums_ref[k : k + 1, :] = jnp.sum(sums[8 * k : 8 * k + 8, :], axis=0, keepdims=True)


def attend_back(dml, qkv, p, wqkv, wo, dqkv, dmix):
    width = wo.shape[0]
    scale = HEAD**-0.5
    dmix[...] = dot_nt(dml, wo[...]).astype(BF16)
    mlo, mhi, low = half_masks()
    tiles = tile_list(dml.shape[0], width)
    d_outs = [block_diag(tile(dmix, t), mlo, mhi) for t in tiles]
    d_ps = [dot_nt(tile(qkv, t, 2, width), d) for t, d in zip(tiles, d_outs)]
    for t, d in zip(tiles, d_outs):
        put_tile(dqkv, t, dot_nn(tile(p, t), d), 2, width)
    d_ss = []
    for t, d_p in zip(tiles, d_ps):
        pf = tile(p, t).astype(F32)
        g = pf * d_p
        d_ss.append((g - pf * jnp.sum(g, axis=0, keepdims=True)).astype(BF16))
    for t, d_s in zip(tiles, d_ss):
        put_tile(
            dqkv, t, dot_nn(d_s, block_diag(tile(qkv, t, 0, width), mlo, mhi)) * scale, 1, width
        )
    both = [dot_tn(d_s, tile(qkv, t, 1, width)) for t, d_s in zip(tiles, d_ss)]
    for t, r in zip(tiles, both):
        put_tile(dqkv, t, jnp.where(low, r[:LEN], r[LEN:]) * scale)
    return dot_nn(dqkv[...], wqkv[...])


def back_own(
    dml, n_one, mix, qkv, p, own, dn1_ref, grad_ref, sums_ref,
    wqkv, wo, dqkv, dmix, acc, acc_out, sums,
):
    @pl.when(pl.program_id(0) == 0)
    def _():
        load_own(own, wqkv, wo)
        acc[...] = jnp.zeros_like(acc)
        acc_out[...] = jnp.zeros_like(acc_out)

    dn1_ref[...] = attend_back(dml[...], qkv, p, wqkv, wo, dqkv, dmix)
    acc[...] += dot_tn(n_one[...], dqkv[...])
    acc_out[...] += dot_tn(dml[...], mix[...])
    add_sums(sums, sums_ref, (dqkv[...].astype(F32),))

    @pl.when(pl.program_id(0) == pl.num_programs(0) - 1)
    def _():
        hc = HEADS * HEAD
        width = wo.shape[0]
        for t in range(3):
            grad_ref[:, t * hc : (t + 1) * hc] = acc[:, t * width : t * width + hc].astype(BF16)
        grad_ref[:, 3 * hc :] = acc_out[:, :hc].astype(BF16)


def back_rest(
    core, tok, time, dml, dmid, dn1, vecs, qkv, p, mine, other,
    gtok_ref, sent_ref, sums_ref, wqkv, wo, dqkv, dmix, sums,
):
    @pl.when(pl.program_id(0) == 0)
    def _():
        load_rest(core[0], mine, other, wqkv, wo)

    d_n = dn1[...] + attend_back(dml[...], qkv, p, wqkv, wo, dqkv, dmix)
    xhat, inv = normed(entry_of(tok, time))
    d_entry = dmid[...] + norm_back(d_n, vecs[0:1, :], xhat, inv)
    gtok_ref[...] = d_entry.astype(BF16)
    sent_ref[...] = jnp.sum(d_entry.reshape(d_entry.shape[0] // LEN, LEN, -1), axis=1)
    add_sums(sums, sums_ref, (d_n * xhat, d_n))


def call(kernel, grid, in_specs, out_specs, out_shape, scratch, slots, args):
    if slots is None:
        return pl.pallas_call(
            kernel, grid=grid, in_specs=in_specs, out_specs=out_specs, out_shape=out_shape,
            scratch_shapes=scratch, compiler_params=params(),
        )(*args)
    return pl.pallas_call(
        kernel,
        grid_spec=pltpu.PrefetchScalarGridSpec(
            num_scalar_prefetch=1, grid=grid, in_specs=in_specs, out_specs=out_specs,
            scratch_shapes=scratch,
        ),
        out_shape=out_shape,
        compiler_params=params(),
    )(slots, *args)


def body(
    tokens, timesteps, time_table, w_qkv, b_qv, w_out, b_out, w_in, b_in, w_back, b_back,
    gain_one, shift_one, gain_two, shift_two, cotangent,
):
    sentences = timesteps.shape[0]
    rows, dim = tokens.shape
    hc = w_out.shape[0]
    hid = w_back.shape[0]
    table_cols = time_table.shape[1]
    n_tensor = dim // hc
    me = lax.axis_index("tensor")
    part = lax.axis_index("dp")
    dp = lax.axis_size("dp")
    order = (me ^ jnp.arange(n_tensor, dtype=jnp.int32)).astype(jnp.int32)
    fast = dp == 8 and n_tensor == 4
    sds = jax.ShapeDtypeStruct

    att_own = jnp.concatenate(
        [jnp.transpose(w_qkv, (1, 2, 0)).reshape(3 * hc, dim), w_out], axis=0
    )
    n_att = att_own.shape[0] // dp
    att_piece = lax.dynamic_slice_in_dim(att_own, part * n_att, n_att, 0)
    if fast:
        core = (part % 2).astype(jnp.int32).reshape(1)
        mine, other = spread(att_piece)
    else:
        core = jnp.zeros((1,), jnp.int32)
        mine, other = spread_any(att_piece, order, dp)
    wi_own = w_in.T
    mlp_shard = jnp.concatenate([wi_own, w_back], axis=0)
    n_mlp = mlp_shard.shape[0] // dp
    mlp_all = lax.all_gather(
        lax.dynamic_slice_in_dim(mlp_shard, part * n_mlp, n_mlp, 0),
        ("tensor", "dp"), axis=0, tiled=True,
    ).reshape(n_tensor, mlp_shard.shape[0], dim)

    steps_iota = lax.broadcasted_iota(jnp.int32, (sentences, time_table.shape[0]), 1)
    picked = timesteps[:, None] == steps_iota
    own_rows = jnp.dot(picked.astype(BF16), time_table, preferred_element_type=F32)
    bias_count = 2 + hid // hc
    shared = lax.all_gather(
        jnp.concatenate(
            [own_rows, b_qv, b_in.reshape(-1, hc), jnp.zeros((-bias_count % 8, hc), F32)]
        ),
        "tensor", axis=0,
    )
    time_rows = jnp.transpose(shared[:, :sentences], (1, 0, 2)).reshape(sentences, dim)
    biases = picked_rows(shared[:, sentences:], order[1:])
    wide = 128 * (-(-3 * hc // 128))
    pad = jnp.zeros((wide - 3 * hc,), F32)
    bias_rest = jnp.concatenate(
        [biases[:, 0].reshape(-1), pad, jnp.zeros((wide,), F32), biases[:, 1].reshape(-1), pad]
    ).reshape(1, 3 * wide)
    bi_rest = biases[:, 2:bias_count].reshape(3, hid)
    thin = 128 * (-(-hc // 128))
    gap = jnp.zeros((thin - hc,), F32)
    bias_own = jnp.concatenate([b_qv[0], gap, jnp.zeros((thin,), F32), b_qv[1], gap])
    vecs = jnp.stack(
        [gain_one, shift_one, gain_two, shift_two, b_out, b_back, b_in, bias_own]
    )

    nb = rows // BR
    grid = (nb,)
    time_spec = rows_spec(dim, BR // LEN)
    vec = whole_spec((8, dim))
    own_spec = whole_spec((4 * hc, dim))
    piece_spec = whole_spec(mine.shape)
    own_scr = [pltpu.VMEM((3 * thin, dim), BF16), pltpu.VMEM((thin, dim), BF16)]
    rest_scr = [pltpu.VMEM((3 * wide, dim), BF16), pltpu.VMEM((wide, dim), BF16)]

    n_one, qkv_a, p_a, mix_a, attn_part = call(
        attend_own, grid,
        [rows_spec(dim), time_spec, vec, own_spec],
        [rows_spec(dim), rows_spec(3 * thin), rows_spec(thin), rows_spec(thin), rows_spec(dim)],
        [sds((rows, dim), BF16), sds((rows, 3 * thin), BF16), sds((rows, thin), BF16),
         sds((rows, thin), BF16), sds((rows, dim), F32)],
        own_scr, None,
        (tokens, time_rows, vecs, att_own),
    )
    qkv_b, p_b, middle, n_two = call(
        attend_rest, grid,
        [rows_spec(dim), time_spec, rows_spec(dim), rows_spec(dim), vec, piece_spec, piece_spec,
         whole_spec((1, 3 * wide))],
        [rows_spec(3 * wide), rows_spec(wide), rows_spec(dim), rows_spec(dim)],
        [sds((rows, 3 * wide), BF16), sds((rows, wide), BF16), sds((rows, dim), F32),
         sds((rows, dim), BF16)],
        rest_scr + [pltpu.VMEM((BR, wide), BF16)], core,
        (tokens, time_rows, n_one, attn_part, vecs, mine, other, bias_rest),
    )
    out_acc, dn2_acc, mlp_grads, gbin = call(
        mlp_own, grid,
        [rows_spec(dim), rows_spec(dim), whole_spec((hid, dim)), whole_spec((hid, dim)), vec],
        [rows_spec(dim), rows_spec(dim), whole_spec((dim, 2 * hid)), whole_spec((1, hid))],
        [sds((rows, dim), F32), sds((rows, dim), F32), sds((dim, 2 * hid), BF16),
         sds((1, hid), F32)],
        [pltpu.VMEM((dim, 2 * hid), F32), pltpu.VMEM((8, hid), F32)], None,
        (n_two, cotangent, wi_own, w_back, vecs),
    )

    def scattered(grad):
        return lax.psum_scatter(grad, "dp", scatter_dimension=0, tiled=True).astype(F32)

    mlp_grads = scattered(mlp_grads)
    mlp_spec = lambda k: slot_spec((2 * hid, dim), k)
    output, d_mid, d_mid_low, sums_two = call(
        mlp_rest, grid,
        [rows_spec(dim), rows_spec(dim), rows_spec(dim), rows_spec(dim), rows_spec(dim), vec,
         mlp_spec(1), mlp_spec(2), mlp_spec(3), whole_spec((3, hid))],
        [rows_spec(dim), rows_spec(dim), rows_spec(dim), whole_spec((4, dim))],
        [sds((rows, dim), BF16), sds((rows, dim), F32), sds((rows, dim), BF16),
         sds((4, dim), F32)],
        [pltpu.VMEM((32, dim), F32)], order,
        (n_two, cotangent, middle, out_acc, dn2_acc, vecs, mlp_all, mlp_all, mlp_all, bi_rest),
    )
    back = lambda w: [pltpu.VMEM((BR, 3 * w), BF16), pltpu.VMEM((BR, w), BF16)]
    dn1_acc, att_grads, sums_qkv = call(
        back_own, grid,
        [rows_spec(dim), rows_spec(dim), rows_spec(thin), rows_spec(3 * thin), rows_spec(thin),
         own_spec],
        [rows_spec(dim), whole_spec((dim, 4 * hc)), whole_spec((1, 3 * thin))],
        [sds((rows, dim), F32), sds((dim, 4 * hc), BF16), sds((1, 3 * thin), F32)],
        own_scr + back(thin)
        + [pltpu.VMEM((dim, 3 * thin), F32), pltpu.VMEM((dim, thin), F32),
           pltpu.VMEM((8, 3 * thin), F32)],
        None,
        (d_mid_low, n_one, mix_a, qkv_a, p_a, att_own),
    )
    att_grads = scattered(att_grads)
    grad_tokens, per_sentence, sums_one = call(
        back_rest, grid,
        [rows_spec(dim), time_spec, rows_spec(dim), rows_spec(dim), rows_spec(dim), vec,
         rows_spec(3 * wide), rows_spec(wide), piece_spec, piece_spec],
        [rows_spec(dim), time_spec, whole_spec((2, dim))],
        [sds((rows, dim), BF16), sds((sentences, dim), F32), sds((2, dim), F32)],
        rest_scr + back(wide) + [pltpu.VMEM((16, dim), F32)], core,
        (tokens, time_rows, d_mid_low, d_mid, dn1_acc, vecs, qkv_b, p_b, mine, other),
    )
    grad_win = mlp_grads[:, :hid]
    grad_wback = mlp_grads[:, hid:].T
    grad_wqkv = att_grads[:, : 3 * hc].reshape(-1, 3, hc)
    grad_wout = att_grads[:, 3 * hc :].T

    bias_row = jnp.concatenate(
        [sums_qkv[:, :thin], timesteps.astype(F32).reshape(1, -1),
         sums_qkv[:, thin + sentences :]], axis=1
    )
    terms = jnp.concatenate([per_sentence, sums_two, sums_one, gbin, bias_row], axis=0)
    terms = lax.all_gather(terms, "dp", axis=0)
    all_cols = lax.dynamic_slice_in_dim(
        terms[:, :sentences], me * table_cols, table_cols, 2
    ).reshape(-1, table_cols)
    small = jnp.sum(terms[:, sentences:], axis=0)
    all_steps = terms[:, -1, thin : thin + sentences].astype(jnp.int32).reshape(-1)
    all_picked = all_steps[:, None] == lax.broadcasted_iota(
        jnp.int32, (all_steps.shape[0], time_table.shape[0]), 1
    )
    grad_table = lax.dot_general(
        all_picked.astype(F32), all_cols, (((0,), (0,)), ((), ())),
        precision=HIGHEST_PREC, preferred_element_type=F32,
    )
    grad_bqv = jnp.stack([small[7, :hc], small[7, 2 * thin : 2 * thin + hc]])
    return (
        output, grad_tokens, grad_table, grad_wqkv, grad_bqv, grad_wout, small[2], grad_win,
        small[6], grad_wback, small[3], small[4], small[5], small[0], small[1],
    )


def picked_rows(array, order):
    return jnp.concatenate(
        [lax.dynamic_slice_in_dim(array, order[k], 1, 0) for k in range(order.shape[0])]
    )


def flipped(n, bits):
    return [(i, i ^ bits) for i in range(n)]


def spread(piece):
    slots = jnp.stack([lax.ppermute(piece, "tensor", flipped(4, k)) for k in (1, 2, 3)])
    whole = jnp.broadcast_to(slots[None], (4,) + slots.shape)
    mine = lax.all_to_all(
        whole, "dp", 0, 0, tiled=True, axis_index_groups=[[0, 2, 4, 6], [1, 3, 5, 7]]
    )
    return mine, lax.ppermute(mine, "dp", flipped(8, 1))


def spread_any(piece, order, dp):
    shards = lax.all_gather(piece, ("tensor", "dp"), axis=0, tiled=True)
    n_tensor = order.shape[0]
    rows = piece.shape[0] * dp
    shards = picked_rows(shards.reshape(n_tensor, rows, -1), order[1:])
    shards = shards.reshape(n_tensor - 1, 4, 2, rows // 8, -1)
    return tuple(jnp.transpose(shards[:, :, c], (1, 0, 2, 3)) for c in (0, 1))


def solution(mesh):
    return jax.shard_map(
        body,
        mesh=mesh,
        in_specs=(
            P("dp", None), P("dp"), P(None, "tensor"), P(None, None, "tensor"), P(None, "tensor"),
            P("tensor", None), P(), P(None, "tensor"), P("tensor"), P("tensor", None), P(), P(),
            P(), P(), P(), P("dp", None),
        ),
        out_specs=(
            P("dp", None), P("dp", None), P(None, "tensor"), P("dp", None, "tensor"),
            P(None, "tensor"), P("tensor", "dp"), P(), P("dp", "tensor"), P("tensor"),
            P("tensor", "dp"), P(), P(), P(), P(), P(),
        ),
        check_vma=False,
    )
```

```python
import functools

import jax
import jax.numpy as jnp
from jax import lax
from jax.experimental import pallas as pl
from jax.experimental.pallas import tpu as pltpu
from jax.sharding import PartitionSpec as P

HEAD = 64
HEADS = 3
LEN = 64
EPS = 1e-05
BR = 512
VMEM_BYTES = 58 * 1024 * 1024
HIGHEST_PREC = lax.Precision.HIGHEST
F32 = jnp.float32
BF16 = jnp.bfloat16


def dot_nn(a, b):
    return lax.dot_general(a, b, (((1,), (0,)), ((), ())), preferred_element_type=F32)


def dot_nt(a, b):
    return lax.dot_general(a, b, (((1,), (1,)), ((), ())), preferred_element_type=F32)


def dot_tn(a, b):
    return lax.dot_general(a, b, (((0,), (0,)), ((), ())), preferred_element_type=F32)


def cost(out_shape, args, flops):
    size = sum(v.size * v.dtype.itemsize for v in (*args, *out_shape))
    return pl.CostEstimate(flops=int(flops), bytes_accessed=int(size), transcendentals=0)


def params():
    return pltpu.CompilerParams(
        dimension_semantics=("arbitrary",), vmem_limit_bytes=VMEM_BYTES
    )


def rows_spec(width, rows=BR):
    return pl.BlockSpec((rows, width), lambda i, *_: (i, 0))


def whole_spec(shape):
    return pl.BlockSpec(shape, lambda i, *_: (0,) * len(shape), pipeline_mode=pl.Buffered(1))


def slot_spec(shape, k):
    return pl.BlockSpec(
        (1,) + shape, lambda i, s: (s[k],) + (0,) * len(shape), pipeline_mode=pl.Buffered(1)
    )


def normed(x):
    mean = jnp.mean(x, axis=-1, keepdims=True)
    centred = x - mean
    spread = jnp.mean(centred * centred, axis=-1, keepdims=True)
    inv = lax.rsqrt(spread + EPS)
    return centred * inv, inv


def norm_back(d_out, gain, xhat, inv):
    gy = d_out * gain
    m1 = jnp.mean(gy, axis=-1, keepdims=True)
    m2 = jnp.mean(gy * xhat, axis=-1, keepdims=True)
    return inv * (gy - m1 - xhat * m2)


def fold8(x):
    return jnp.sum(x.reshape(x.shape[0] // 8, 8, x.shape[1]), axis=0)


def entry_of(tok_ref, time_ref):
    tok = tok_ref[...].astype(F32)
    n = tok.shape[0] // LEN
    return (tok.reshape(n, LEN, tok.shape[1]) + time_ref[0][:, None, :]).reshape(tok.shape)


def half_masks():
    lane = lax.broadcasted_iota(jnp.int32, (LEN, 2 * HEAD), 1)
    low = (lane < HEAD).astype(F32)
    return low.astype(BF16), (1.0 - low).astype(BF16), lane < HEAD


def block_diag(x, mlo, mhi):
    return jnp.concatenate([x * mlo, x * mhi], axis=0)


def load_own(att, wqkv, wo, s):
    hc = HEADS * HEAD
    for t in range(3):
        wqkv[(2 * t + s) * hc : (2 * t + s + 1) * hc, :] = att[t * hc : (t + 1) * hc, :]
    wo[s * hc : (s + 1) * hc, :] = att[3 * hc :, :]


def load_pieces(core, mine, other, k, wqkv, wo, s):
    hc = HEADS * HEAD
    n = hc // 2
    for src, at in ((mine, core * n), (other, (1 - core) * n)):
        for t in range(3):
            wqkv[pl.ds(pl.multiple_of((2 * t + s) * hc + at, 16), n), :] = src[t, k]
        wo[pl.ds(pl.multiple_of(s * hc + at, 16), n), :] = src[3, k]


def tile_list(rows, width):
    return [(s, j) for s in range(rows // LEN) for j in range(width // 128)]


def tile(ref, st, part=0, width=0):
    s, j = st
    return ref[s * LEN : (s + 1) * LEN, part * width + j * 128 : part * width + (j + 1) * 128]


def put_tile(ref, st, value, part=0, width=0):
    s, j = st
    ref[s * LEN : (s + 1) * LEN, part * width + j * 128 : part * width + (j + 1) * 128] = (
        value.astype(BF16)
    )


def attend(n_one, wqkv, wo, bias, qkv_ref, p_ref, mix_ref):
    width = wo.shape[0]
    qkv_ref[...] = (dot_nt(n_one, wqkv[...]) + bias).astype(BF16)
    mlo, mhi, low = half_masks()
    tiles = tile_list(n_one.shape[0], width)
    scores = [
        dot_nt(tile(qkv_ref, t, 1, width), block_diag(tile(qkv_ref, t, 0, width), mlo, mhi))
        for t in tiles
    ]
    probs = []
    for t, sc in zip(tiles, scores):
        top = jnp.max(sc, axis=0, keepdims=True)
        e = jnp.exp((sc - top) * (HEAD**-0.5))
        p = (e * (1.0 / jnp.sum(e, axis=0, keepdims=True))).astype(BF16)
        probs.append(p)
        put_tile(p_ref, t, p)
    both = [dot_tn(p, tile(qkv_ref, t, 2, width)) for t, p in zip(tiles, probs)]
    for t, r in zip(tiles, both):
        put_tile(mix_ref, t, jnp.where(low, r[:LEN], r[LEN:]))
    return dot_nn(mix_ref[...], wo[...])


def attend_first(
    core, tok, time, vecs, own, mine, other, bias,
    n_one_ref, qkv_ref, p_ref, mix_ref, part_ref, wqkv, wo,
):
    @pl.when(pl.program_id(0) == 0)
    def _():
        load_own(own, wqkv, wo, 0)
        load_pieces(core[0], mine, other, 0, wqkv, wo, 1)

    xhat, _ = normed(entry_of(tok, time))
    n_one = (xhat * vecs[0:1, :] + vecs[1:2, :]).astype(BF16)
    n_one_ref[...] = n_one
    part = attend(n_one, wqkv, wo, bias[0:1, :], qkv_ref, p_ref, mix_ref)
    part_ref[...] = part.astype(part_ref.dtype)


def attend_last(
    core, tok, time, n_one, part, vecs, mine, other, bias,
    qkv_ref, p_ref, middle_ref, n_two_ref, wqkv, wo, mix_ref,
):
    @pl.when(pl.program_id(0) == 0)
    def _():
        load_pieces(core[0], mine, other, 0, wqkv, wo, 0)
        load_pieces(core[0], mine, other, 1, wqkv, wo, 1)

    more = attend(n_one[...], wqkv, wo, bias[1:2, :], qkv_ref, p_ref, mix_ref)
    middle = entry_of(tok, time) + part[...].astype(F32) + more + vecs[4:5, :]
    middle_ref[...] = middle
    xhat, _ = normed(middle)
    n_two_ref[...] = (xhat * vecs[2:3, :] + vecs[3:4, :]).astype(BF16)


ERF_P = 0.3275911
ERF_A = (0.254829592, -0.284496736, 1.421413741, -1.453152027, 1.061405429)


def gelu_both(x):
    bell = jnp.exp(x * x * (-0.5))
    t = 1.0 / (1.0 + jnp.abs(x) * (ERF_P * 0.5**0.5))
    poly = t * (
        0.5 * ERF_A[0]
        + t * (0.5 * ERF_A[1] + t * (0.5 * ERF_A[2] + t * (0.5 * ERF_A[3] + t * (0.5 * ERF_A[4]))))
    )
    tail = poly * bell
    cdf = jnp.where(x >= 0, 1.0 - tail, tail)
    return x * cdf, cdf + x * bell * 0.3989422804014327


def mlp_slot(n_two, c, wi, wb, b):
    pre = dot_nt(n_two, wi) + b
    d_act = dot_nt(c, wb)
    act, slope = gelu_both(pre)
    act = act.astype(BF16)
    d_pre = (d_act * slope).astype(BF16)
    return act, d_pre


def mlp_own(n_two, c, wi, wb, vecs, out_ref, dn2_ref, grad_ref, gbin_ref, acc, sums):
    hid = wi.shape[0]

    @pl.when(pl.program_id(0) == 0)
    def _():
        acc[...] = jnp.zeros_like(acc)
        sums[...] = jnp.zeros_like(sums)

    act, d_pre = mlp_slot(n_two[...], c[...], wi[...], wb[...], vecs[6:7, :])
    sums[...] += fold8(d_pre.astype(F32))
    out_ref[...] = dot_nn(act, wb[...]).astype(BF16)
    dn2_ref[...] = dot_nn(d_pre, wi[...]).astype(BF16)
    acc[:, :hid] += dot_tn(n_two[...], d_pre)
    acc[:, hid:] += dot_tn(c[...], act)

    @pl.when(pl.program_id(0) == pl.num_programs(0) - 1)
    def _():
        grad_ref[...] = acc[...].astype(BF16)
        gbin_ref[...] = jnp.sum(sums[...], axis=0, keepdims=True)


def mlp_rest(
    slots, n_two, c, middle, out_in, dn2_in, vecs, w1, w2, w3, b,
    out_ref, dmid_ref, sums_ref, sums,
):
    hid = b.shape[-1]
    start_sums(sums)
    out = out_in[...].astype(F32)
    dn2 = dn2_in[...].astype(F32)
    for k, w in enumerate((w1, w2, w3)):
        act, d_pre = mlp_slot(
            n_two[...], c[...], w[0, :hid, :], w[0, hid:, :], b[k : k + 1, :]
        )
        out = out + dot_nn(act, w[0, hid:, :])
        dn2 = dn2 + dot_nn(d_pre, w[0, :hid, :])
    mid = middle[...]
    cot = c[...].astype(F32)
    out_ref[...] = (mid + out + vecs[5:6, :]).astype(BF16)
    xhat, inv = normed(mid)
    d_mid = cot + norm_back(dn2, vecs[2:3, :], xhat, inv)
    dmid_ref[...] = d_mid
    add_sums(sums, (dn2 * xhat, dn2, d_mid, cot))
    end_sums(sums, sums_ref)


def start_sums(sums):
    @pl.when(pl.program_id(0) == 0)
    def _():
        sums[...] = jnp.zeros_like(sums)


def add_sums(sums, terms):
    for k, term in enumerate(terms):
        sums[8 * k : 8 * k + 8, :] += fold8(term)


def end_sums(sums, sums_ref):
    @pl.when(pl.program_id(0) == pl.num_programs(0) - 1)
    def _():
        for k in range(sums_ref.shape[0]):
            sums_ref[k : k + 1, :] = jnp.sum(sums[8 * k : 8 * k + 8, :], axis=0, keepdims=True)


def attend_back(dml, qkv, p, wqkv, wo, dqkv, dmix):
    width = wo.shape[0]
    scale = HEAD**-0.5
    dmix[...] = dot_nt(dml, wo[...]).astype(BF16)
    mlo, mhi, low = half_masks()
    tiles = tile_list(dml.shape[0], width)
    d_outs = [block_diag(tile(dmix, t), mlo, mhi) for t in tiles]
    d_ps = [dot_nt(tile(qkv, t, 2, width), d) for t, d in zip(tiles, d_outs)]
    for t, d in zip(tiles, d_outs):
        put_tile(dqkv, t, dot_nn(tile(p, t), d), 2, width)
    d_ss = []
    for t, d_p in zip(tiles, d_ps):
        pf = tile(p, t).astype(F32)
        g = pf * d_p
        d_ss.append((g - pf * jnp.sum(g, axis=0, keepdims=True)).astype(BF16))
    for t, d_s in zip(tiles, d_ss):
        put_tile(
            dqkv, t, dot_nn(d_s, block_diag(tile(qkv, t, 0, width), mlo, mhi)) * scale, 1, width
        )
    both = [dot_tn(d_s, tile(qkv, t, 1, width)) for t, d_s in zip(tiles, d_ss)]
    for t, r in zip(tiles, both):
        put_tile(dqkv, t, jnp.where(low, r[:LEN], r[LEN:]) * scale)
    return dot_nn(dqkv[...], wqkv[...])


def back_first(
    core, dmid, n_one, mix, qkv, p, own, mine, other, dn1_ref, grad_ref, sums_ref,
    wqkv, wo, dqkv, dmix, acc, sums,
):
    @pl.when(pl.program_id(0) == 0)
    def _():
        load_own(own, wqkv, wo, 0)
        load_pieces(core[0], mine, other, 0, wqkv, wo, 1)
        acc[...] = jnp.zeros_like(acc)

    start_sums(sums)
    dml = dmid[...].astype(BF16)
    dn1_ref[...] = attend_back(dml, qkv, p, wqkv, wo, dqkv, dmix).astype(dn1_ref.dtype)
    width = wo.shape[0]
    for t in range(3):
        acc[:, t * 256 : (t + 1) * 256] += dot_tn(
            n_one[...], dqkv[:, t * width : t * width + 256]
        )
    acc[:, 768:] += dot_tn(dml, mix[:, :256])
    add_sums(sums, (dqkv[...].astype(F32),))
    end_sums(sums, sums_ref)

    @pl.when(pl.program_id(0) == pl.num_programs(0) - 1)
    def _():
        hc = HEADS * HEAD
        for t in range(4):
            grad_ref[:, t * hc : (t + 1) * hc] = acc[:, t * 256 : t * 256 + hc].astype(BF16)


def back_last(
    core, tok, time, dmid, dn1, vecs, qkv, p, mine, other, more,
    gtok_ref, terms_ref, wqkv, wo, dqkv, dmix, sums,
):
    @pl.when(pl.program_id(0) == 0)
    def _():
        load_pieces(core[0], mine, other, 0, wqkv, wo, 0)
        load_pieces(core[0], mine, other, 1, wqkv, wo, 1)

    start_sums(sums)
    d_mid = dmid[...]
    d_n = dn1[...].astype(F32) + attend_back(
        d_mid.astype(BF16), qkv, p, wqkv, wo, dqkv, dmix
    )
    xhat, inv = normed(entry_of(tok, time))
    d_entry = d_mid + norm_back(d_n, vecs[0:1, :], xhat, inv)
    gtok_ref[...] = d_entry.astype(BF16)
    n = d_entry.shape[0] // LEN
    at = pl.multiple_of(pl.program_id(0) * n, 8)
    terms_ref[pl.ds(at, n), :] = jnp.sum(d_entry.reshape(n, LEN, -1), axis=1)
    add_sums(sums, (d_n * xhat, d_n))

    @pl.when(pl.program_id(0) == pl.num_programs(0) - 1)
    def _():
        total = n * pl.num_programs(0)
        terms_ref[pl.ds(pl.multiple_of(total, 8), 8), :] = more[...]
        for k in range(2):
            terms_ref[pl.ds(total + 4 + k, 1), :] = jnp.sum(
                sums[8 * k : 8 * k + 8, :], axis=0, keepdims=True
            )


def call(kernel, grid, in_specs, out_specs, out_shape, scratch, slots, args, flops):
    if slots is None:
        return pl.pallas_call(
            kernel, grid=grid, in_specs=in_specs, out_specs=out_specs, out_shape=out_shape,
            scratch_shapes=scratch, compiler_params=params(),
            cost_estimate=cost(out_shape, args, flops),
        )(*args)
    return pl.pallas_call(
        kernel,
        grid_spec=pltpu.PrefetchScalarGridSpec(
            num_scalar_prefetch=1, grid=grid, in_specs=in_specs, out_specs=out_specs,
            scratch_shapes=scratch,
        ),
        out_shape=out_shape,
        compiler_params=params(),
        cost_estimate=cost(out_shape, args, flops),
    )(slots, *args)


def body(
    tokens, timesteps, time_table, w_qkv, b_qv, w_out, b_out, w_in, b_in, w_back, b_back,
    gain_one, shift_one, gain_two, shift_two, cotangent,
):
    sentences = timesteps.shape[0]
    rows, dim = tokens.shape
    hc = w_out.shape[0]
    hid = w_back.shape[0]
    table_cols = time_table.shape[1]
    n_tensor = dim // hc
    me = lax.axis_index("tensor")
    part = lax.axis_index("dp")
    dp = lax.axis_size("dp")
    order = [me ^ k for k in range(n_tensor)]
    fast = dp == 8 and n_tensor == 4
    sds = jax.ShapeDtypeStruct
    nb = rows // BR
    unit = 1e9

    att_own = jnp.concatenate(
        [jnp.transpose(w_qkv, (1, 2, 0)).reshape(3 * hc, dim), w_out], axis=0
    )
    n_att = att_own.shape[0] // dp
    att_piece = lax.dynamic_slice_in_dim(att_own, part * n_att, n_att, 0)

    steps_iota = lax.broadcasted_iota(jnp.int32, (sentences, time_table.shape[0]), 1)
    picked = timesteps[:, None] == steps_iota
    own_rows = jnp.dot(picked.astype(BF16), time_table, preferred_element_type=F32)
    bias_count = 2 + hid // hc
    own_bias = jnp.concatenate([b_qv, b_in.reshape(-1, hc)])
    if fast:
        core = (part % 2).astype(jnp.int32).reshape(1)
        planes = jnp.pad(three(own_bias), ((0, sentences - 3 * bias_count), (0, 0)))
        note = jnp.concatenate(
            [own_rows.astype(BF16), jnp.zeros((sentences, 256 - hc), BF16), planes,
             jnp.zeros((sentences, dim - 256 - hc), BF16)], axis=1
        )
        message = jnp.concatenate([att_piece, note])
        got = [lax.ppermute(message, "tensor", flipped(4, k)) for k in (1, 2, 3)]
        mine_a = spread_plane([got[0][:n_att]])
        mine_b = spread_plane([got[1][:n_att], got[2][:n_att]])
        other_a = lax.ppermute(mine_a, "dp", flipped(8, 1))
        time_slots = jnp.stack([own_rows] + [m[n_att:, :hc].astype(F32) for m in got])
        bias_slots = jnp.stack(
            [own_bias] + [of_three(m[n_att:, 256 : 256 + hc], bias_count) for m in got]
        )
    else:
        core = jnp.zeros((1,), jnp.int32)
        (mine_a, mine_b), (other_a, other_b) = spread_any(att_piece, order, dp)
        time_slots = picked_rows(lax.all_gather(own_rows, "tensor", axis=0), order)
        bias_slots = picked_rows(lax.all_gather(own_bias, "tensor", axis=0), order)

    wi_own = w_in.T
    mlp_shard = jnp.concatenate([wi_own, w_back], axis=0)
    n_mlp = mlp_shard.shape[0] // dp
    mlp_all = lax.all_gather(
        lax.dynamic_slice_in_dim(mlp_shard, part * n_mlp, n_mlp, 0),
        ("tensor", "dp"), axis=0, tiled=True,
    ).reshape(n_tensor, mlp_shard.shape[0], dim)

    time_rows = jnp.transpose(picked_rows(time_slots, order), (1, 0, 2))
    time_rows = time_rows.reshape(nb, BR // LEN, dim)
    bq, bv = bias_slots[:, 0].reshape(2, -1), bias_slots[:, 1].reshape(2, -1)
    bias_rows = jnp.concatenate([bq, jnp.zeros_like(bq), bv], axis=1)
    bi_rest = bias_slots[1:, 2:].reshape(3, hid)
    zero = jnp.zeros_like(b_out)
    vecs = jnp.stack([gain_one, shift_one, gain_two, shift_two, b_out, b_back, b_in, zero])

    grid = (nb,)
    width = 2 * hc
    time_spec = pl.BlockSpec((1, BR // LEN, dim), lambda i, *_: (i, 0, 0))
    vec = whole_spec((8, dim))
    own_spec = whole_spec((4 * hc, dim))
    piece_spec = lambda k: whole_spec((4, k, hc // 2, dim))
    bias_spec = whole_spec((2, 3 * width))
    weights = [pltpu.VMEM((3 * width, dim), BF16), pltpu.VMEM((width, dim), BF16)]
    back = [pltpu.VMEM((BR, 3 * width), BF16), pltpu.VMEM((BR, width), BF16)]

    n_one, qkv_a, p_a, mix_a, attn_part = call(
        attend_first, grid,
        [rows_spec(dim), time_spec, vec, own_spec, piece_spec(1), piece_spec(1), bias_spec],
        [rows_spec(dim), rows_spec(3 * width), rows_spec(width), rows_spec(width),
         rows_spec(dim)],
        [sds((rows, dim), BF16), sds((rows, 3 * width), BF16), sds((rows, width), BF16),
         sds((rows, width), BF16), sds((rows, dim), BF16)],
        weights, core,
        (tokens, time_rows, vecs, att_own, mine_a, other_a, bias_rows), 14 * unit,
    )
    if fast:
        mine_b, n_one = lax.optimization_barrier((mine_b, n_one))
        other_b = lax.ppermute(mine_b, "dp", flipped(8, 1))
    qkv_b, p_b, middle, n_two = call(
        attend_last, grid,
        [rows_spec(dim), time_spec, rows_spec(dim), rows_spec(dim), vec, piece_spec(2),
         piece_spec(2), bias_spec],
        [rows_spec(3 * width), rows_spec(width), rows_spec(dim), rows_spec(dim)],
        [sds((rows, 3 * width), BF16), sds((rows, width), BF16), sds((rows, dim), F32),
         sds((rows, dim), BF16)],
        weights + [pltpu.VMEM((BR, width), BF16)], core,
        (tokens, time_rows, n_one, attn_part, vecs, mine_b, other_b, bias_rows), 15 * unit,
    )
    out_acc, dn2_acc, mlp_grads, gbin = call(
        mlp_own, grid,
        [rows_spec(dim), rows_spec(dim), whole_spec((hid, dim)), whole_spec((hid, dim)), vec],
        [rows_spec(dim), rows_spec(dim), whole_spec((dim, 2 * hid)), whole_spec((1, hid))],
        [sds((rows, dim), BF16), sds((rows, dim), BF16), sds((dim, 2 * hid), BF16),
         sds((1, hid), F32)],
        [pltpu.VMEM((dim, 2 * hid), F32), pltpu.VMEM((8, hid), F32)], None,
        (n_two, cotangent, wi_own, w_back, vecs), 21 * unit,
    )

    def scattered(grad):
        return lax.psum_scatter(grad, "dp", scatter_dimension=0, tiled=True)

    mlp_grads, mlp_all = lax.optimization_barrier((mlp_grads, mlp_all))
    mlp_grads = scattered(mlp_grads)
    mlp_spec = lambda k: slot_spec((2 * hid, dim), k)
    output, d_mid, sums_two = call(
        mlp_rest, grid,
        [rows_spec(dim), rows_spec(dim), rows_spec(dim), rows_spec(dim), rows_spec(dim), vec,
         mlp_spec(1), mlp_spec(2), mlp_spec(3), whole_spec((3, hid))],
        [rows_spec(dim), rows_spec(dim), whole_spec((4, dim))],
        [sds((rows, dim), BF16), sds((rows, dim), F32), sds((4, dim), F32)],
        [pltpu.VMEM((32, dim), F32)], me ^ jnp.arange(n_tensor, dtype=jnp.int32),
        (n_two, cotangent, middle, out_acc, dn2_acc, vecs, mlp_all, mlp_all, mlp_all, bi_rest),
        44 * unit,
    )
    dn1_acc, att_grads, sums_qkv = call(
        back_first, grid,
        [rows_spec(dim), rows_spec(dim), rows_spec(width), rows_spec(3 * width),
         rows_spec(width), own_spec, piece_spec(1), piece_spec(1)],
        [rows_spec(dim), whole_spec((dim, 4 * hc)), whole_spec((1, 3 * width))],
        [sds((rows, dim), BF16), sds((dim, 4 * hc), BF16), sds((1, 3 * width), F32)],
        weights + back
        + [pltpu.VMEM((dim, 1024), F32), pltpu.VMEM((8, 3 * width), F32)],
        core,
        (d_mid, n_one, mix_a, qkv_a, p_a, att_own, mine_a, other_a), 18 * unit,
    )
    if fast:
        parts = lax.all_to_all(
            att_grads.reshape(dp, dim // dp, 4 * hc), "dp", 0, 0, tiled=True
        )
    else:
        att_grads = scattered(att_grads).astype(F32)
    bias_row = jnp.concatenate(
        [sums_qkv[:, :256], timesteps.astype(F32).reshape(1, -1),
         jnp.zeros((1, dim - 512 - sentences), F32), sums_qkv[:, 2 * width : 2 * width + 256]],
        axis=1,
    )
    more = jnp.concatenate([sums_two, jnp.zeros((2, dim), F32), gbin, bias_row])
    grad_win = mlp_grads[:, :hid].astype(F32)
    grad_wback = mlp_grads[:, hid:].astype(F32).T
    dn1_acc, grad_win, grad_wback = lax.optimization_barrier((dn1_acc, grad_win, grad_wback))
    grad_tokens, terms = call(
        back_last, grid,
        [rows_spec(dim), time_spec, rows_spec(dim), rows_spec(dim), vec,
         rows_spec(3 * width), rows_spec(width), piece_spec(2), piece_spec(2), vec],
        [rows_spec(dim), whole_spec((sentences + 8, dim))],
        [sds((rows, dim), BF16), sds((sentences + 8, dim), F32)],
        weights + back + [pltpu.VMEM((16, dim), F32)], core,
        (tokens, time_rows, d_mid, dn1_acc, vecs, qkv_b, p_b, mine_b, other_b, more), 20 * unit,
    )
    if fast:
        terms, parts = lax.optimization_barrier((terms, parts))
        att_grads = jnp.sum(parts.astype(F32), axis=0)
    terms = lax.all_gather(terms, "dp", axis=0)
    all_cols = lax.dynamic_slice_in_dim(
        terms[:, :sentences], me * table_cols, table_cols, 2
    ).reshape(-1, table_cols)
    small = jnp.sum(terms[:, sentences:], axis=0)
    all_steps = terms[:, -1, 256 : 256 + sentences].astype(jnp.int32).reshape(-1)
    all_picked = all_steps[:, None] == lax.broadcasted_iota(
        jnp.int32, (all_steps.shape[0], time_table.shape[0]), 1
    )
    grad_table = lax.dot_general(
        all_picked.astype(F32), all_cols, (((0,), (0,)), ((), ())),
        precision=HIGHEST_PREC, preferred_element_type=F32,
    )
    grad_wqkv = att_grads[:, : 3 * hc].reshape(-1, 3, hc)
    grad_wout = att_grads[:, 3 * hc :].T
    grad_bqv = jnp.stack([small[7, :hc], small[7, dim - 256 : dim - 256 + hc]])
    return (
        output, grad_tokens, grad_table, grad_wqkv, grad_bqv, grad_wout, small[2], grad_win,
        small[6], grad_wback, small[3], small[4], small[5], small[0], small[1],
    )


def picked_rows(array, order):
    return jnp.concatenate([lax.dynamic_slice_in_dim(array, k, 1, 0) for k in order])


def three(value):
    parts = []
    for _ in range(3):
        low = lax.reduce_precision(value, 8, 7)
        parts.append(low.astype(BF16))
        value = value - low
    return jnp.concatenate(parts)


def of_three(rows, n):
    rows = rows.astype(F32)
    return (rows[2 * n : 3 * n] + rows[n : 2 * n]) + rows[:n]


def flipped(n, bits):
    return [(i, i ^ bits) for i in range(n)]


def spread_plane(slots):
    slots = jnp.stack(slots)
    whole = jnp.broadcast_to(slots[None], (4,) + slots.shape)
    return lax.all_to_all(
        whole, "dp", 0, 0, tiled=True, axis_index_groups=[[0, 2, 4, 6], [1, 3, 5, 7]]
    )


def spread_any(piece, order, dp):
    shards = lax.all_gather(piece, ("tensor", "dp"), axis=0, tiled=True)
    n_tensor = len(order)
    rows = piece.shape[0] * dp
    shards = picked_rows(shards.reshape(n_tensor, rows, -1), order[1:])
    shards = shards.reshape(n_tensor - 1, 4, 2, rows // 8, -1)
    halves = [jnp.transpose(shards[:, :, c], (1, 0, 2, 3)) for c in (0, 1)]
    return tuple((h[:, :1], h[:, 1:]) for h in halves)


def solution(mesh):
    return jax.shard_map(
        body,
        mesh=mesh,
        in_specs=(
            P("dp", None), P("dp"), P(None, "tensor"), P(None, None, "tensor"), P(None, "tensor"),
            P("tensor", None), P(), P(None, "tensor"), P("tensor"), P("tensor", None), P(), P(),
            P(), P(), P(), P("dp", None),
        ),
        out_specs=(
            P("dp", None), P("dp", None), P(None, "tensor"), P("dp", None, "tensor"),
            P(None, "tensor"), P("tensor", "dp"), P(), P("dp", "tensor"), P("tensor"),
            P("tensor", "dp"), P(), P(), P(), P(), P(),
        ),
        check_vma=False,
    )
```

```python
import functools

import jax
import jax.numpy as jnp
from jax import lax
from jax.experimental import pallas as pl
from jax.experimental.pallas import tpu as pltpu
from jax.sharding import PartitionSpec as P

HEAD = 64
HEADS = 3
LEN = 64
EPS = 1e-05
BR = 512
VMEM_BYTES = 58 * 1024 * 1024
HIGHEST_PREC = lax.Precision.HIGHEST
F32 = jnp.float32
BF16 = jnp.bfloat16


def dot_nn(a, b):
    return lax.dot_general(a, b, (((1,), (0,)), ((), ())), preferred_element_type=F32)


def dot_nt(a, b):
    return lax.dot_general(a, b, (((1,), (1,)), ((), ())), preferred_element_type=F32)


def dot_tn(a, b):
    return lax.dot_general(a, b, (((0,), (0,)), ((), ())), preferred_element_type=F32)


def cost(out_shape, args, flops):
    size = sum(v.size * v.dtype.itemsize for v in (*args, *out_shape))
    return pl.CostEstimate(flops=int(flops), bytes_accessed=int(size), transcendentals=0)


def params():
    return pltpu.CompilerParams(
        dimension_semantics=("arbitrary",), vmem_limit_bytes=VMEM_BYTES
    )


def rows_spec(width, rows=BR):
    return pl.BlockSpec((rows, width), lambda i, *_: (i, 0))


def whole_spec(shape):
    return pl.BlockSpec(shape, lambda i, *_: (0,) * len(shape), pipeline_mode=pl.Buffered(1))


def slot_spec(shape, k):
    return pl.BlockSpec(
        (1,) + shape, lambda i, s: (s[k],) + (0,) * len(shape), pipeline_mode=pl.Buffered(1)
    )


def normed(x):
    mean = jnp.mean(x, axis=-1, keepdims=True)
    centred = x - mean
    spread = jnp.mean(centred * centred, axis=-1, keepdims=True)
    inv = lax.rsqrt(spread + EPS)
    return centred * inv, inv


def norm_back(d_out, gain, xhat, inv):
    gy = d_out * gain
    m1 = jnp.mean(gy, axis=-1, keepdims=True)
    m2 = jnp.mean(gy * xhat, axis=-1, keepdims=True)
    return inv * (gy - m1 - xhat * m2)


def fold8(x):
    return jnp.sum(x.reshape(x.shape[0] // 8, 8, x.shape[1]), axis=0)


def entry_of(tok_ref, time_ref):
    tok = tok_ref[...].astype(F32)
    n = tok.shape[0] // LEN
    return (tok.reshape(n, LEN, tok.shape[1]) + time_ref[0][:, None, :]).reshape(tok.shape)


def half_masks():
    lane = lax.broadcasted_iota(jnp.int32, (LEN, 2 * HEAD), 1)
    low = (lane < HEAD).astype(F32)
    return low.astype(BF16), (1.0 - low).astype(BF16), lane < HEAD


def block_diag(x, mlo, mhi):
    return jnp.concatenate([x * mlo, x * mhi], axis=0)


def load_own(att, wqkv, wo, s):
    hc = HEADS * HEAD
    for t in range(3):
        wqkv[(2 * t + s) * hc : (2 * t + s + 1) * hc, :] = att[t * hc : (t + 1) * hc, :]
    wo[s * hc : (s + 1) * hc, :] = att[3 * hc :, :]


def load_pieces(core, mine, other, k, wqkv, wo, s):
    hc = HEADS * HEAD
    n = hc // 2
    for src, at in ((mine, core * n), (other, (1 - core) * n)):
        for t in range(3):
            wqkv[pl.ds(pl.multiple_of((2 * t + s) * hc + at, 16), n), :] = src[t, k]
        wo[pl.ds(pl.multiple_of(s * hc + at, 16), n), :] = src[3, k]


def tile_list(rows, width):
    return [(s, j) for s in range(rows // LEN) for j in range(width // 128)]


def tile(ref, st, part=0, width=0):
    s, j = st
    return ref[s * LEN : (s + 1) * LEN, part * width + j * 128 : part * width + (j + 1) * 128]


def put_tile(ref, st, value, part=0, width=0):
    s, j = st
    ref[s * LEN : (s + 1) * LEN, part * width + j * 128 : part * width + (j + 1) * 128] = (
        value.astype(BF16)
    )


def attend(n_one, wqkv, wo, bias, qkv_ref, p_ref, mix_ref):
    width = wo.shape[0]
    qkv_ref[...] = (dot_nt(n_one, wqkv[...]) + bias).astype(BF16)
    mlo, mhi, low = half_masks()
    tiles = tile_list(n_one.shape[0], width)
    scores = [
        dot_nt(tile(qkv_ref, t, 1, width), block_diag(tile(qkv_ref, t, 0, width), mlo, mhi))
        for t in tiles
    ]
    probs = []
    for t, sc in zip(tiles, scores):
        top = jnp.max(sc, axis=0, keepdims=True)
        e = jnp.exp((sc - top) * (HEAD**-0.5))
        p = (e * (1.0 / jnp.sum(e, axis=0, keepdims=True))).astype(BF16)
        probs.append(p)
        put_tile(p_ref, t, p)
    both = [dot_tn(p, tile(qkv_ref, t, 2, width)) for t, p in zip(tiles, probs)]
    for t, r in zip(tiles, both):
        put_tile(mix_ref, t, jnp.where(low, r[:LEN], r[LEN:]))
    return dot_nn(mix_ref[...], wo[...])


def attend_first(
    core, tok, time, vecs, own, mine, other, bias,
    n_one_ref, qkv_ref, p_ref, mix_ref, part_ref, wqkv, wo,
):
    @pl.when(pl.program_id(0) == 0)
    def _():
        load_own(own, wqkv, wo, 0)
        load_pieces(core[0], mine, other, 0, wqkv, wo, 1)

    xhat, _ = normed(entry_of(tok, time))
    n_one = (xhat * vecs[0:1, :] + vecs[1:2, :]).astype(BF16)
    n_one_ref[...] = n_one
    part = attend(n_one, wqkv, wo, bias[0:1, :], qkv_ref, p_ref, mix_ref)
    part_ref[...] = part.astype(part_ref.dtype)


def attend_last(
    core, tok, time, n_one, part, vecs, mine, other, bias,
    qkv_ref, p_ref, middle_ref, n_two_ref, wqkv, wo, mix_ref,
):
    @pl.when(pl.program_id(0) == 0)
    def _():
        load_pieces(core[0], mine, other, 0, wqkv, wo, 0)
        load_pieces(core[0], mine, other, 1, wqkv, wo, 1)

    more = attend(n_one[...], wqkv, wo, bias[1:2, :], qkv_ref, p_ref, mix_ref)
    middle = entry_of(tok, time) + part[...].astype(F32) + more + vecs[4:5, :]
    middle_ref[...] = middle
    xhat, _ = normed(middle)
    n_two_ref[...] = (xhat * vecs[2:3, :] + vecs[3:4, :]).astype(BF16)


ERF_P = 0.3275911
ERF_A = (0.254829592, -0.284496736, 1.421413741, -1.453152027, 1.061405429)


def gelu_both(x):
    bell = jnp.exp(x * x * (-0.5))
    t = 1.0 / (1.0 + jnp.abs(x) * (ERF_P * 0.5**0.5))
    poly = t * (
        0.5 * ERF_A[0]
        + t * (0.5 * ERF_A[1] + t * (0.5 * ERF_A[2] + t * (0.5 * ERF_A[3] + t * (0.5 * ERF_A[4]))))
    )
    tail = poly * bell
    cdf = jnp.where(x >= 0, 1.0 - tail, tail)
    return x * cdf, cdf + x * bell * 0.3989422804014327


def mlp_slot(n_two, c, wi, wb, b):
    pre = dot_nn(n_two, wi) + b
    d_act = dot_nt(c, wb)
    act, slope = gelu_both(pre)
    act = act.astype(BF16)
    d_pre = (d_act * slope).astype(BF16)
    return act, d_pre


def mlp_own(n_two, c, wi, wb, vecs, out_ref, dn2_ref, grad_ref, gbin_ref, acc, sums):
    hid = wb.shape[0]

    @pl.when(pl.program_id(0) == 0)
    def _():
        acc[...] = jnp.zeros_like(acc)
        sums[...] = jnp.zeros_like(sums)

    act, d_pre = mlp_slot(n_two[...], c[...], wi[...], wb[...], vecs[6:7, :])
    sums[...] += fold8(d_pre.astype(F32))
    out_ref[...] = dot_nn(act, wb[...]).astype(BF16)
    dn2_ref[...] = dot_nt(d_pre, wi[...]).astype(BF16)
    acc[:, :hid] += dot_tn(n_two[...], d_pre)
    acc[:, hid:] += dot_tn(c[...], act)

    @pl.when(pl.program_id(0) == pl.num_programs(0) - 1)
    def _():
        grad_ref[...] = acc[...].astype(BF16)
        gbin_ref[...] = jnp.sum(sums[...], axis=0, keepdims=True)


def total(rows):
    return jnp.sum(rows, axis=0, keepdims=True)


def start_sums(sums):
    @pl.when(pl.program_id(0) == 0)
    def _():
        sums[...] = jnp.zeros_like(sums)


def add_sums(sums, terms):
    for k, term in enumerate(terms):
        sums[8 * k : 8 * k + 8, :] += fold8(term)


def end_sums(sums, sums_ref):
    @pl.when(pl.program_id(0) == pl.num_programs(0) - 1)
    def _():
        for k in range(sums_ref.shape[0]):
            sums_ref[k : k + 1, :] = jnp.sum(sums[8 * k : 8 * k + 8, :], axis=0, keepdims=True)


def attend_back(dml, qkv, p, wqkv, wo, dqkv, dmix):
    width = wo.shape[0]
    scale = HEAD**-0.5
    dmix[...] = dot_nt(dml, wo[...]).astype(BF16)
    mlo, mhi, low = half_masks()
    tiles = tile_list(dml.shape[0], width)
    d_outs = [block_diag(tile(dmix, t), mlo, mhi) for t in tiles]
    d_ps = [dot_nt(tile(qkv, t, 2, width), d) for t, d in zip(tiles, d_outs)]
    for t, d in zip(tiles, d_outs):
        put_tile(dqkv, t, dot_nn(tile(p, t), d), 2, width)
    d_ss = []
    for t, d_p in zip(tiles, d_ps):
        pf = tile(p, t).astype(F32)
        g = pf * d_p
        d_ss.append((g - pf * jnp.sum(g, axis=0, keepdims=True)).astype(BF16))
    for t, d_s in zip(tiles, d_ss):
        put_tile(
            dqkv, t, dot_nn(d_s, block_diag(tile(qkv, t, 0, width), mlo, mhi)) * scale, 1, width
        )
    both = [dot_tn(d_s, tile(qkv, t, 1, width)) for t, d_s in zip(tiles, d_ss)]
    for t, r in zip(tiles, both):
        put_tile(dqkv, t, jnp.where(low, r[:LEN], r[LEN:]) * scale)
    return dot_nn(dqkv[...], wqkv[...])


def rest_and_back(
    slots, n_two, c, middle, out_in, dn2_in, vecs, w1, w2, w3, b,
    n_one, mix, qkv, p, own, mine, other, gbin, steps,
    out_ref, dmid_ref, dn1_ref, grad_ref, more_ref,
    sums, wqkv, wo, dqkv, dmix, acc, bias_sums,
):
    @pl.when(pl.program_id(0) == 0)
    def _():
        load_own(own, wqkv, wo, 0)
        load_pieces(slots[4], mine, other, 0, wqkv, wo, 1)
        acc[...] = jnp.zeros_like(acc)

    start_sums(sums)
    start_sums(bias_sums)

    dim = n_two.shape[1]
    out = out_in[...].astype(F32)
    dn2 = dn2_in[...].astype(F32)
    for k, w in enumerate((w1, w2, w3)):
        act, d_pre = mlp_slot(
            n_two[...], c[...], w[0, :dim, :], w[0, dim:, :], b[k : k + 1, :]
        )
        out = out + dot_nn(act, w[0, dim:, :])
        dn2 = dn2 + dot_nt(d_pre, w[0, :dim, :])
    mid = middle[...]
    cot = c[...].astype(F32)
    out_ref[...] = (mid + out + vecs[5:6, :]).astype(BF16)
    xhat, inv = normed(mid)
    d_mid = cot + norm_back(dn2, vecs[2:3, :], xhat, inv)
    dmid_ref[...] = d_mid
    add_sums(sums, (dn2 * xhat, dn2, d_mid, cot))

    dml = d_mid.astype(BF16)
    dn1_ref[...] = attend_back(dml, qkv, p, wqkv, wo, dqkv, dmix).astype(dn1_ref.dtype)
    width = wo.shape[0]
    for t in range(3):
        acc[:, t * 256 : (t + 1) * 256] += dot_tn(
            n_one[...], dqkv[:, t * width : t * width + 256]
        )
    acc[:, 768:] += dot_tn(dml, mix[:, :256])
    add_sums(bias_sums, (dqkv[...].astype(F32),))

    @pl.when(pl.program_id(0) == pl.num_programs(0) - 1)
    def _():
        for r in range(4):
            more_ref[r : r + 1, :] = total(sums[8 * r : 8 * r + 8, :])
        more_ref[4:6, :] = jnp.zeros_like(more_ref[4:6, :])
        more_ref[6:7, :] = gbin[...]
        more_ref[7:8, :] = steps[...]
        bias = total(bias_sums[...])
        more_ref[7:8, :256] = bias[:, :256]
        more_ref[7:8, 512:] = bias[:, 2 * width : 2 * width + 256]
        hc = HEADS * HEAD
        for t in range(4):
            grad_ref[:, t * hc : (t + 1) * hc] = acc[:, t * 256 : t * 256 + hc].astype(BF16)


def back_last(
    places, tok, time, dmid, dn1, vecs, qkv, p, mine, other, more, mlp_sums,
    gtok_ref, terms_ref, gwin_ref, gwback_ref, wqkv, wo, dqkv, dmix, sums, per,
):
    @pl.when(pl.program_id(0) == 0)
    def _():
        load_pieces(places[4], mine, other, 0, wqkv, wo, 0)
        load_pieces(places[4], mine, other, 1, wqkv, wo, 1)
        hid = gwin_ref.shape[1]
        gwin_ref[...] = mlp_sums[:, :hid].astype(F32)
        gwback_ref[...] = mlp_sums[:, hid:].astype(F32)

    start_sums(sums)
    d_mid = dmid[...]
    d_n = dn1[...].astype(F32) + attend_back(
        d_mid.astype(BF16), qkv, p, wqkv, wo, dqkv, dmix
    )
    xhat, inv = normed(entry_of(tok, time))
    d_entry = d_mid + norm_back(d_n, vecs[0:1, :], xhat, inv)
    gtok_ref[...] = d_entry.astype(BF16)
    n = d_entry.shape[0] // LEN
    at = pl.multiple_of(pl.program_id(0) * n, 8)
    per[pl.ds(at, n), :] = jnp.sum(d_entry.reshape(n, LEN, -1), axis=1)
    add_sums(sums, (d_n * xhat, d_n))

    @pl.when(pl.program_id(0) == pl.num_programs(0) - 1)
    def _():
        cols = per.shape[1] // 4
        own = per[:, :cols]
        for j in range(1, 4):
            own = jnp.where(places[0] == j, per[:, j * cols : (j + 1) * cols], own)
        for j in range(4):
            terms_ref[0, :8, j * cols : (j + 1) * cols] = own[8 * j : 8 * j + 8, :]
        terms_ref[0, 8:12, :] = more[0:4, :]
        terms_ref[0, 12:13, :] = total(sums[0:8, :])
        terms_ref[0, 13:14, :] = total(sums[8:16, :])
        terms_ref[0, 14:16, :] = more[6:8, :]
        for k in range(1, terms_ref.shape[0]):
            terms_ref[k] = terms_ref[0]


def call(kernel, grid, in_specs, out_specs, out_shape, scratch, slots, args, flops):
    if slots is None:
        return pl.pallas_call(
            kernel, grid=grid, in_specs=in_specs, out_specs=out_specs, out_shape=out_shape,
            scratch_shapes=scratch, compiler_params=params(),
            cost_estimate=cost(out_shape, args, flops),
        )(*args)
    return pl.pallas_call(
        kernel,
        grid_spec=pltpu.PrefetchScalarGridSpec(
            num_scalar_prefetch=1, grid=grid, in_specs=in_specs, out_specs=out_specs,
            scratch_shapes=scratch,
        ),
        out_shape=out_shape,
        compiler_params=params(),
        cost_estimate=cost(out_shape, args, flops),
    )(slots, *args)


def body(
    tokens, timesteps, time_table, w_qkv, b_qv, w_out, b_out, w_in, b_in, w_back, b_back,
    gain_one, shift_one, gain_two, shift_two, cotangent,
):
    sentences = timesteps.shape[0]
    rows, dim = tokens.shape
    hc = w_out.shape[0]
    hid = w_back.shape[0]
    table_cols = time_table.shape[1]
    n_tensor = dim // hc
    me = lax.axis_index("tensor")
    part = lax.axis_index("dp")
    dp = lax.axis_size("dp")
    order = [me ^ k for k in range(n_tensor)]
    fast = dp == 8 and n_tensor == 4
    sds = jax.ShapeDtypeStruct
    nb = rows // BR
    unit = 1e9

    att_own = jnp.concatenate(
        [jnp.transpose(w_qkv, (1, 2, 0)).reshape(3 * hc, dim), w_out], axis=0
    )
    n_att = att_own.shape[0] // dp
    att_piece = lax.dynamic_slice_in_dim(att_own, part * n_att, n_att, 0)

    steps_iota = lax.broadcasted_iota(jnp.int32, (sentences, time_table.shape[0]), 1)
    picked = timesteps[:, None] == steps_iota
    own_rows = jnp.dot(picked.astype(BF16), time_table, preferred_element_type=F32)
    bias_count = 2 + hid // hc
    own_bias = jnp.concatenate([b_qv, b_in.reshape(-1, hc)])
    if fast:
        core = (part % 2).astype(jnp.int32).reshape(1)
        planes = jnp.pad(three(own_bias), ((0, sentences - 3 * bias_count), (0, 0)))
        note = jnp.concatenate(
            [own_rows.astype(BF16), jnp.zeros((sentences, 256 - hc), BF16), planes,
             jnp.zeros((sentences, dim - 256 - hc), BF16)], axis=1
        )
        message = jnp.concatenate([att_piece, note])
        got = [lax.ppermute(message, "tensor", flipped(4, k)) for k in (1, 2, 3)]
        mine_a = spread_plane([got[0][:n_att]])
        mine_b = spread_plane([got[1][:n_att], got[2][:n_att]])
        other_a = lax.ppermute(mine_a, "dp", flipped(8, 1))
        time_slots = jnp.stack([own_rows] + [m[n_att:, :hc].astype(F32) for m in got])
        bias_slots = jnp.stack(
            [own_bias] + [of_three(m[n_att:, 256 : 256 + hc], bias_count) for m in got]
        )
    else:
        core = jnp.zeros((1,), jnp.int32)
        (mine_a, mine_b), (other_a, other_b) = spread_any(att_piece, order, dp)
        time_slots = picked_rows(lax.all_gather(own_rows, "tensor", axis=0), order)
        bias_slots = picked_rows(lax.all_gather(own_bias, "tensor", axis=0), order)

    n_mlp = (dim + hid) // dp
    if fast:
        first = dim // n_mlp
        up = lax.dynamic_slice_in_dim(w_in, jnp.minimum(part, first - 1) * n_mlp, n_mlp, 0)
        down = lax.dynamic_slice_in_dim(w_back, jnp.maximum(part - first, 0) * n_mlp, n_mlp, 0)
        mlp_piece = jnp.where(part < first, up, down)
    else:
        mlp_piece = lax.dynamic_slice_in_dim(
            jnp.concatenate([w_in, w_back]), part * n_mlp, n_mlp, 0
        )
    mlp_all = lax.all_gather(mlp_piece, ("tensor", "dp"), axis=0, tiled=True)
    mlp_all = mlp_all.reshape(n_tensor, dim + hid, dim)

    time_rows = jnp.concatenate([time_slots[k] for k in range(n_tensor)], axis=1)
    for bit in range(n_tensor.bit_length() - 1):
        step = hc << bit
        swapped = jnp.concatenate(
            [time_rows[:, (j ^ 1) * step : ((j ^ 1) + 1) * step] for j in range(dim // step)],
            axis=1,
        )
        time_rows = jnp.where((me >> bit) % 2 == 1, swapped, time_rows)
    time_rows = time_rows.reshape(nb, BR // LEN, dim)
    bq, bv = bias_slots[:, 0].reshape(2, -1), bias_slots[:, 1].reshape(2, -1)
    bias_rows = jnp.concatenate([bq, jnp.zeros_like(bq), bv], axis=1)
    bi_rest = bias_slots[1:, 2:].reshape(3, hid)
    zero = jnp.zeros_like(b_out)
    vecs = jnp.stack([gain_one, shift_one, gain_two, shift_two, b_out, b_back, b_in, zero])

    grid = (nb,)
    width = 2 * hc
    time_spec = pl.BlockSpec((1, BR // LEN, dim), lambda i, *_: (i, 0, 0))
    vec = whole_spec((8, dim))
    own_spec = whole_spec((4 * hc, dim))
    piece_spec = lambda k: whole_spec((4, k, hc // 2, dim))
    bias_spec = whole_spec((2, 3 * width))
    weights = [pltpu.VMEM((3 * width, dim), BF16), pltpu.VMEM((width, dim), BF16)]
    back = [pltpu.VMEM((BR, 3 * width), BF16), pltpu.VMEM((BR, width), BF16)]

    n_one, qkv_a, p_a, mix_a, attn_part = call(
        attend_first, grid,
        [rows_spec(dim), time_spec, vec, own_spec, piece_spec(1), piece_spec(1), bias_spec],
        [rows_spec(dim), rows_spec(3 * width), rows_spec(width), rows_spec(width),
         rows_spec(dim)],
        [sds((rows, dim), BF16), sds((rows, 3 * width), BF16), sds((rows, width), BF16),
         sds((rows, width), BF16), sds((rows, dim), BF16)],
        weights, core,
        (tokens, time_rows, vecs, att_own, mine_a, other_a, bias_rows), 14 * unit,
    )
    if fast:
        mine_b, n_one = lax.optimization_barrier((mine_b, n_one))
        other_b = lax.ppermute(mine_b, "dp", flipped(8, 1))
    qkv_b, p_b, middle, n_two = call(
        attend_last, grid,
        [rows_spec(dim), time_spec, rows_spec(dim), rows_spec(dim), vec, piece_spec(2),
         piece_spec(2), bias_spec],
        [rows_spec(3 * width), rows_spec(width), rows_spec(dim), rows_spec(dim)],
        [sds((rows, 3 * width), BF16), sds((rows, width), BF16), sds((rows, dim), F32),
         sds((rows, dim), BF16)],
        weights + [pltpu.VMEM((BR, width), BF16)], core,
        (tokens, time_rows, n_one, attn_part, vecs, mine_b, other_b, bias_rows), 15 * unit,
    )
    out_acc, dn2_acc, mlp_grads, gbin = call(
        mlp_own, grid,
        [rows_spec(dim), rows_spec(dim), whole_spec((dim, hid)), whole_spec((hid, dim)), vec],
        [rows_spec(dim), rows_spec(dim), whole_spec((dim, 2 * hid)), whole_spec((1, hid))],
        [sds((rows, dim), BF16), sds((rows, dim), BF16), sds((dim, 2 * hid), BF16),
         sds((1, hid), F32)],
        [pltpu.VMEM((dim, 2 * hid), F32), pltpu.VMEM((8, hid), F32)], None,
        (n_two, cotangent, w_in, w_back, vecs), 21 * unit,
    )

    def scattered(grad):
        return lax.psum_scatter(grad, "dp", scatter_dimension=0, tiled=True)

    mlp_grads, mlp_all = lax.optimization_barrier((mlp_grads, mlp_all))
    mlp_grads = scattered(mlp_grads)
    mlp_spec = lambda k: slot_spec((dim + hid, dim), k)
    places = jnp.concatenate([me ^ jnp.arange(n_tensor, dtype=jnp.int32), core])
    spread_steps = jnp.pad(timesteps.astype(F32), (256, dim - 256 - sentences)).reshape(1, dim)
    output, d_mid, dn1_acc, att_grads, more = call(
        rest_and_back, grid,
        [rows_spec(dim), rows_spec(dim), rows_spec(dim), rows_spec(dim), rows_spec(dim), vec,
         mlp_spec(1), mlp_spec(2), mlp_spec(3), whole_spec((3, hid)),
         rows_spec(dim), rows_spec(width), rows_spec(3 * width), rows_spec(width), own_spec,
         piece_spec(1), piece_spec(1), whole_spec((1, dim)), whole_spec((1, dim))],
        [rows_spec(dim), rows_spec(dim), rows_spec(dim), whole_spec((dim, 4 * hc)), vec],
        [sds((rows, dim), BF16), sds((rows, dim), F32), sds((rows, dim), BF16),
         sds((dim, 4 * hc), BF16), sds((8, dim), F32)],
        [pltpu.VMEM((32, dim), F32)] + weights + back
        + [pltpu.VMEM((dim, 1024), F32), pltpu.VMEM((8, 3 * width), F32)],
        places,
        (n_two, cotangent, middle, out_acc, dn2_acc, vecs, mlp_all, mlp_all, mlp_all, bi_rest,
         n_one, mix_a, qkv_a, p_a, att_own, mine_a, other_a, gbin, spread_steps),
        62 * unit,
    )
    copies = dp if fast else 1
    if fast:
        parts = lax.all_to_all(
            att_grads.reshape(dp, dim // dp, 4 * hc), "dp", 0, 0, tiled=True
        )
    else:
        att_grads = scattered(att_grads).astype(F32)
    grad_tokens, terms, grad_win, grad_wback = call(
        back_last, grid,
        [rows_spec(dim), time_spec, rows_spec(dim), rows_spec(dim), vec,
         rows_spec(3 * width), rows_spec(width), piece_spec(2), piece_spec(2), vec,
         whole_spec(mlp_grads.shape)],
        [rows_spec(dim), whole_spec((copies, 16, dim)),
         whole_spec((dim // dp, hid)), whole_spec((dim // dp, hid))],
        [sds((rows, dim), BF16), sds((copies, 16, dim), F32),
         sds((dim // dp, hid), F32), sds((dim // dp, hid), F32)],
        weights + back + [pltpu.VMEM((16, dim), F32), pltpu.VMEM((sentences, dim), F32)],
        places,
        (tokens, time_rows, d_mid, dn1_acc, vecs, qkv_b, p_b, mine_b, other_b, more, mlp_grads),
        20 * unit,
    )

    if fast:
        terms, parts = lax.optimization_barrier((terms, parts))
        terms = lax.all_to_all(terms, "dp", 0, 0, tiled=True)
    else:
        terms = lax.all_gather(terms, "dp", axis=0, tiled=True)
    if fast:
        att_grads = jnp.sum(parts.astype(F32), axis=0)
    grad_wqkv = att_grads[:, : 3 * hc].reshape(-1, 3, hc)
    grad_wout = att_grads[:, 3 * hc :].T
    all_cols = terms[:, :8].reshape(-1, table_cols)
    small = jnp.sum(terms[:, 8:], axis=0)
    all_steps = terms[:, -1, 256 : 256 + sentences].astype(jnp.int32)
    all_steps = jnp.transpose(all_steps.reshape(dp, 4, 8), (0, 2, 1)).reshape(-1)
    all_picked = all_steps[:, None] == lax.broadcasted_iota(
        jnp.int32, (all_steps.shape[0], time_table.shape[0]), 1
    )
    grad_table = lax.dot_general(
        all_picked.astype(F32), all_cols, (((0,), (0,)), ((), ())),
        precision=HIGHEST_PREC, preferred_element_type=F32,
    )
    grad_bqv = jnp.stack([small[7, :hc], small[7, dim - 256 : dim - 256 + hc]])
    return (
        output, grad_tokens, grad_table, grad_wqkv, grad_bqv, grad_wout, small[2], grad_win,
        small[6], grad_wback.T, small[3], small[4], small[5], small[0], small[1],
    )


def picked_rows(array, order):
    return jnp.concatenate([lax.dynamic_slice_in_dim(array, k, 1, 0) for k in order])


def three(value):
    parts = []
    for _ in range(3):
        low = lax.reduce_precision(value, 8, 7)
        parts.append(low.astype(BF16))
        value = value - low
    return jnp.concatenate(parts)


def of_three(rows, n):
    rows = rows.astype(F32)
    return (rows[2 * n : 3 * n] + rows[n : 2 * n]) + rows[:n]


def flipped(n, bits):
    return [(i, i ^ bits) for i in range(n)]


def spread_plane(slots):
    slots = jnp.stack(slots)
    whole = jnp.broadcast_to(slots[None], (4,) + slots.shape)
    return lax.all_to_all(
        whole, "dp", 0, 0, tiled=True, axis_index_groups=[[0, 2, 4, 6], [1, 3, 5, 7]]
    )


def spread_any(piece, order, dp):
    shards = lax.all_gather(piece, ("tensor", "dp"), axis=0, tiled=True)
    n_tensor = len(order)
    rows = piece.shape[0] * dp
    shards = picked_rows(shards.reshape(n_tensor, rows, -1), order[1:])
    shards = shards.reshape(n_tensor - 1, 4, 2, rows // 8, -1)
    halves = [jnp.transpose(shards[:, :, c], (1, 0, 2, 3)) for c in (0, 1)]
    return tuple((h[:, :1], h[:, 1:]) for h in halves)


def solution(mesh):
    return jax.shard_map(
        body,
        mesh=mesh,
        in_specs=(
            P("dp", None), P("dp"), P(None, "tensor"), P(None, None, "tensor"), P(None, "tensor"),
            P("tensor", None), P(), P(None, "tensor"), P("tensor"), P("tensor", None), P(), P(),
            P(), P(), P(), P("dp", None),
        ),
        out_specs=(
            P("dp", None), P("dp", None), P(None, "tensor"), P("dp", None, "tensor"),
            P(None, "tensor"), P("tensor", "dp"), P(), P("dp", "tensor"), P("tensor"),
            P("tensor", "dp"), P(), P(), P(), P(), P(),
        ),
        check_vma=False,
    )
```

```python
import functools

import jax
import jax.numpy as jnp
from jax import lax
from jax.experimental import pallas as pl
from jax.experimental.pallas import tpu as pltpu
from jax.sharding import PartitionSpec as P

HEAD = 64
HEADS = 3
LEN = 64
EPS = 1e-05
BR = 512
VMEM_BYTES = 58 * 1024 * 1024
HIGHEST_PREC = lax.Precision.HIGHEST
F32 = jnp.float32
BF16 = jnp.bfloat16


def dot_nn(a, b):
    return lax.dot_general(a, b, (((1,), (0,)), ((), ())), preferred_element_type=F32)


def dot_nt(a, b):
    return lax.dot_general(a, b, (((1,), (1,)), ((), ())), preferred_element_type=F32)


def dot_tn(a, b):
    return lax.dot_general(a, b, (((0,), (0,)), ((), ())), preferred_element_type=F32)


def cost(out_shape, args, flops):
    size = sum(v.size * v.dtype.itemsize for v in (*args, *out_shape))
    return pl.CostEstimate(flops=int(flops), bytes_accessed=int(size), transcendentals=0)


def params():
    return pltpu.CompilerParams(
        dimension_semantics=("arbitrary",), vmem_limit_bytes=VMEM_BYTES
    )


def rows_spec(width, rows=BR):
    return pl.BlockSpec((rows, width), lambda i, *_: (i, 0))


def whole_spec(shape):
    return pl.BlockSpec(shape, lambda i, *_: (0,) * len(shape), pipeline_mode=pl.Buffered(1))


def slot_spec(shape, k):
    return pl.BlockSpec(
        (1,) + shape, lambda i, s: (s[k],) + (0,) * len(shape), pipeline_mode=pl.Buffered(1)
    )


def normed(x):
    mean = jnp.mean(x, axis=-1, keepdims=True)
    centred = x - mean
    spread = jnp.mean(centred * centred, axis=-1, keepdims=True)
    inv = lax.rsqrt(spread + EPS)
    return centred * inv, inv


def norm_back(d_out, gain, xhat, inv):
    gy = d_out * gain
    m1 = jnp.mean(gy, axis=-1, keepdims=True)
    m2 = jnp.mean(gy * xhat, axis=-1, keepdims=True)
    return inv * (gy - m1 - xhat * m2)


def fold8(x):
    return jnp.sum(x.reshape(x.shape[0] // 8, 8, x.shape[1]), axis=0)


def entry_of(tok_ref, time_ref):
    tok = tok_ref[...].astype(F32)
    n = tok.shape[0] // LEN
    return (tok.reshape(n, LEN, tok.shape[1]) + time_ref[0][:, None, :]).reshape(tok.shape)


def half_masks():
    lane = lax.broadcasted_iota(jnp.int32, (LEN, 2 * HEAD), 1)
    low = (lane < HEAD).astype(F32)
    return low.astype(BF16), (1.0 - low).astype(BF16), lane < HEAD


def block_diag(x, mlo, mhi):
    return jnp.concatenate([x * mlo, x * mhi], axis=0)


def load_own(att, wqkv, wo, s):
    hc = HEADS * HEAD
    for t in range(3):
        wqkv[(2 * t + s) * hc : (2 * t + s + 1) * hc, :] = att[t * hc : (t + 1) * hc, :]
    wo[s * hc : (s + 1) * hc, :] = att[3 * hc :, :]


def load_pieces(core, mine, other, k, wqkv, wo, s):
    hc = HEADS * HEAD
    n = hc // 2
    for src, at in ((mine, core * n), (other, (1 - core) * n)):
        for t in range(3):
            wqkv[pl.ds(pl.multiple_of((2 * t + s) * hc + at, 16), n), :] = src[t, k]
        wo[pl.ds(pl.multiple_of(s * hc + at, 16), n), :] = src[3, k]


def tile_list(rows, width):
    return [(s, j) for s in range(rows // LEN) for j in range(width // 128)]


def tile(ref, st, part=0, width=0):
    s, j = st
    return ref[s * LEN : (s + 1) * LEN, part * width + j * 128 : part * width + (j + 1) * 128]


def put_tile(ref, st, value, part=0, width=0):
    s, j = st
    ref[s * LEN : (s + 1) * LEN, part * width + j * 128 : part * width + (j + 1) * 128] = (
        value.astype(BF16)
    )


def attend(n_one, wqkv, wo, bias, qkv_ref, p_ref, mix_ref):
    width = wo.shape[0]
    qkv_ref[...] = (dot_nt(n_one, wqkv[...]) + bias).astype(BF16)
    mlo, mhi, low = half_masks()
    tiles = tile_list(n_one.shape[0], width)
    scores = [
        dot_nt(tile(qkv_ref, t, 1, width), block_diag(tile(qkv_ref, t, 0, width), mlo, mhi))
        for t in tiles
    ]
    probs = []
    for t, sc in zip(tiles, scores):
        top = jnp.max(sc, axis=0, keepdims=True)
        e = jnp.exp((sc - top) * (HEAD**-0.5))
        p = (e * (1.0 / jnp.sum(e, axis=0, keepdims=True))).astype(BF16)
        probs.append(p)
        put_tile(p_ref, t, p)
    both = [dot_tn(p, tile(qkv_ref, t, 2, width)) for t, p in zip(tiles, probs)]
    for t, r in zip(tiles, both):
        put_tile(mix_ref, t, jnp.where(low, r[:LEN], r[LEN:]))
    return dot_nn(mix_ref[...], wo[...])


def attend_first(
    core, tok, time, vecs, own, mine, other, bias,
    n_one_ref, qkv_ref, p_ref, mix_ref, part_ref, wqkv, wo,
):
    @pl.when(pl.program_id(0) == 0)
    def _():
        load_own(own, wqkv, wo, 0)
        load_pieces(core[0], mine, other, 0, wqkv, wo, 1)

    xhat, _ = normed(entry_of(tok, time))
    n_one = (xhat * vecs[0:1, :] + vecs[1:2, :]).astype(BF16)
    n_one_ref[...] = n_one
    part = attend(n_one, wqkv, wo, bias[0:1, :], qkv_ref, p_ref, mix_ref)
    part_ref[...] = part.astype(part_ref.dtype)


def attend_last(
    core, tok, time, n_one, part, vecs, mine, other, bias,
    qkv_ref, p_ref, middle_ref, n_two_ref, wqkv, wo, mix_ref,
):
    @pl.when(pl.program_id(0) == 0)
    def _():
        load_pieces(core[0], mine, other, 0, wqkv, wo, 0)
        load_pieces(core[0], mine, other, 1, wqkv, wo, 1)

    more = attend(n_one[...], wqkv, wo, bias[1:2, :], qkv_ref, p_ref, mix_ref)
    middle = entry_of(tok, time) + part[...].astype(F32) + more + vecs[4:5, :]
    middle_ref[...] = middle
    xhat, _ = normed(middle)
    n_two_ref[...] = (xhat * vecs[2:3, :] + vecs[3:4, :]).astype(BF16)


ERF_P = 0.3275911
ERF_A = (0.254829592, -0.284496736, 1.421413741, -1.453152027, 1.061405429)


def gelu_both(x):
    bell = jnp.exp(x * x * (-0.5))
    t = 1.0 / (1.0 + jnp.abs(x) * (ERF_P * 0.5**0.5))
    poly = t * (
        0.5 * ERF_A[0]
        + t * (0.5 * ERF_A[1] + t * (0.5 * ERF_A[2] + t * (0.5 * ERF_A[3] + t * (0.5 * ERF_A[4]))))
    )
    tail = poly * bell
    cdf = jnp.where(x >= 0, 1.0 - tail, tail)
    return x * cdf, cdf + x * bell * 0.3989422804014327


def mlp_slot(n_two, c, wi, wb, b):
    pre = dot_nn(n_two, wi) + b
    d_act = dot_nt(c, wb)
    act, slope = gelu_both(pre)
    act = act.astype(BF16)
    d_pre = (d_act * slope).astype(BF16)
    return act, d_pre


def mlp_own(n_two, c, wi, wb, vecs, out_ref, dn2_ref, grad_ref, gbin_ref, acc, sums):
    hid = wb.shape[0]

    @pl.when(pl.program_id(0) == 0)
    def _():
        acc[...] = jnp.zeros_like(acc)
        sums[...] = jnp.zeros_like(sums)

    act, d_pre = mlp_slot(n_two[...], c[...], wi[...], wb[...], vecs[6:7, :])
    sums[...] += fold8(d_pre.astype(F32))
    out_ref[...] = dot_nn(act, wb[...]).astype(BF16)
    dn2_ref[...] = dot_nt(d_pre, wi[...]).astype(BF16)
    acc[:, :hid] += dot_tn(n_two[...], d_pre)
    acc[:, hid:] += dot_tn(c[...], act)

    @pl.when(pl.program_id(0) == pl.num_programs(0) - 1)
    def _():
        grad_ref[...] = acc[...].astype(BF16)
        gbin_ref[...] = jnp.sum(sums[...], axis=0, keepdims=True)


def total(rows):
    return jnp.sum(rows, axis=0, keepdims=True)


def start_sums(sums):
    @pl.when(pl.program_id(0) == 0)
    def _():
        sums[...] = jnp.zeros_like(sums)


def add_sums(sums, terms):
    for k, term in enumerate(terms):
        sums[8 * k : 8 * k + 8, :] += fold8(term)


def end_sums(sums, sums_ref):
    @pl.when(pl.program_id(0) == pl.num_programs(0) - 1)
    def _():
        for k in range(sums_ref.shape[0]):
            sums_ref[k : k + 1, :] = jnp.sum(sums[8 * k : 8 * k + 8, :], axis=0, keepdims=True)


def attend_back(dml, qkv, p, wqkv, wo, dqkv, dmix):
    width = wo.shape[0]
    scale = HEAD**-0.5
    dmix[...] = dot_nt(dml, wo[...]).astype(BF16)
    mlo, mhi, low = half_masks()
    tiles = tile_list(dml.shape[0], width)
    d_outs = [block_diag(tile(dmix, t), mlo, mhi) for t in tiles]
    d_ps = [dot_nt(tile(qkv, t, 2, width), d) for t, d in zip(tiles, d_outs)]
    for t, d in zip(tiles, d_outs):
        put_tile(dqkv, t, dot_nn(tile(p, t), d), 2, width)
    d_ss = []
    for t, d_p in zip(tiles, d_ps):
        pf = tile(p, t).astype(F32)
        g = pf * d_p
        d_ss.append((g - pf * jnp.sum(g, axis=0, keepdims=True)).astype(BF16))
    for t, d_s in zip(tiles, d_ss):
        put_tile(
            dqkv, t, dot_nn(d_s, block_diag(tile(qkv, t, 0, width), mlo, mhi)) * scale, 1, width
        )
    both = [dot_tn(d_s, tile(qkv, t, 1, width)) for t, d_s in zip(tiles, d_ss)]
    for t, r in zip(tiles, both):
        put_tile(dqkv, t, jnp.where(low, r[:LEN], r[LEN:]) * scale)
    return dot_nn(dqkv[...], wqkv[...])


def rest_and_back(
    slots, n_two, c, middle, out_in, dn2_in, vecs, w1, w2, w3, b,
    n_one, mix, qkv, p, own, mine, other, gbin, steps,
    out_ref, dmid_ref, dn1_ref, grad_ref, more_ref,
    sums, wqkv, wo, dqkv, dmix, acc, bias_sums,
):
    @pl.when(pl.program_id(0) == 0)
    def _():
        load_own(own, wqkv, wo, 0)
        load_pieces(slots[4], mine, other, 0, wqkv, wo, 1)
        acc[...] = jnp.zeros_like(acc)

    start_sums(sums)
    start_sums(bias_sums)

    dim = n_two.shape[1]
    out = out_in[...].astype(F32)
    dn2 = dn2_in[...].astype(F32)
    for k, w in enumerate((w1, w2, w3)):
        act, d_pre = mlp_slot(
            n_two[...], c[...], w[0, :dim, :], w[0, dim:, :], b[k : k + 1, :]
        )
        out = out + dot_nn(act, w[0, dim:, :])
        dn2 = dn2 + dot_nt(d_pre, w[0, :dim, :])
    mid = middle[...]
    cot = c[...].astype(F32)
    out_ref[...] = (mid + out + vecs[5:6, :]).astype(BF16)
    xhat, inv = normed(mid)
    d_mid = cot + norm_back(dn2, vecs[2:3, :], xhat, inv)
    add_sums(sums, (dn2 * xhat, dn2, d_mid, cot))

    dml = d_mid.astype(BF16)
    dmid_ref[...] = dml
    dn1_ref[...] = attend_back(dml, qkv, p, wqkv, wo, dqkv, dmix).astype(dn1_ref.dtype)
    width = wo.shape[0]
    for t in range(3):
        acc[:, t * 256 : (t + 1) * 256] += dot_tn(
            n_one[...], dqkv[:, t * width : t * width + 256]
        )
    acc[:, 768:] += dot_tn(dml, mix[:, :256])
    add_sums(bias_sums, (dqkv[...].astype(F32),))

    @pl.when(pl.program_id(0) == pl.num_programs(0) - 1)
    def _():
        for r in range(4):
            more_ref[r : r + 1, :] = total(sums[8 * r : 8 * r + 8, :])
        more_ref[4:6, :] = jnp.zeros_like(more_ref[4:6, :])
        more_ref[6:7, :] = gbin[...]
        more_ref[7:8, :] = steps[...]
        bias = total(bias_sums[...])
        more_ref[7:8, :256] = bias[:, :256]
        more_ref[7:8, 512:] = bias[:, 2 * width : 2 * width + 256]
        hc = HEADS * HEAD
        for t in range(4):
            grad_ref[:, t * hc : (t + 1) * hc] = acc[:, t * 256 : t * 256 + hc].astype(BF16)


def back_last(
    places, tok, time, dmid, dn1, vecs, qkv, p, mine, other, more, mlp_sums,
    gtok_ref, terms_ref, gwin_ref, gwback_ref, wqkv, wo, dqkv, dmix, sums, per,
):
    @pl.when(pl.program_id(0) == 0)
    def _():
        load_pieces(places[4], mine, other, 0, wqkv, wo, 0)
        load_pieces(places[4], mine, other, 1, wqkv, wo, 1)
        hid = gwin_ref.shape[1]
        gwin_ref[...] = mlp_sums[:, :hid].astype(F32)
        gwback_ref[...] = mlp_sums[:, hid:].astype(F32)

    start_sums(sums)
    d_n = dn1[...].astype(F32) + attend_back(dmid[...], qkv, p, wqkv, wo, dqkv, dmix)
    xhat, inv = normed(entry_of(tok, time))
    d_entry = dmid[...].astype(F32) + norm_back(d_n, vecs[0:1, :], xhat, inv)
    gtok_ref[...] = d_entry.astype(BF16)
    n = d_entry.shape[0] // LEN
    at = pl.multiple_of(pl.program_id(0) * n, 8)
    per[pl.ds(at, n), :] = jnp.sum(d_entry.reshape(n, LEN, -1), axis=1)
    add_sums(sums, (d_n * xhat, d_n))

    @pl.when(pl.program_id(0) == pl.num_programs(0) - 1)
    def _():
        cols = per.shape[1] // 4
        own = per[:, :cols]
        for j in range(1, 4):
            own = jnp.where(places[0] == j, per[:, j * cols : (j + 1) * cols], own)
        for j in range(4):
            terms_ref[0, :8, j * cols : (j + 1) * cols] = own[8 * j : 8 * j + 8, :]
        terms_ref[0, 8:12, :] = more[0:4, :]
        terms_ref[0, 12:13, :] = total(sums[0:8, :])
        terms_ref[0, 13:14, :] = total(sums[8:16, :])
        terms_ref[0, 14:16, :] = more[6:8, :]
        for k in range(1, terms_ref.shape[0]):
            terms_ref[k] = terms_ref[0]


def call(kernel, grid, in_specs, out_specs, out_shape, scratch, slots, args, flops):
    if slots is None:
        return pl.pallas_call(
            kernel, grid=grid, in_specs=in_specs, out_specs=out_specs, out_shape=out_shape,
            scratch_shapes=scratch, compiler_params=params(),
            cost_estimate=cost(out_shape, args, flops),
        )(*args)
    return pl.pallas_call(
        kernel,
        grid_spec=pltpu.PrefetchScalarGridSpec(
            num_scalar_prefetch=1, grid=grid, in_specs=in_specs, out_specs=out_specs,
            scratch_shapes=scratch,
        ),
        out_shape=out_shape,
        compiler_params=params(),
        cost_estimate=cost(out_shape, args, flops),
    )(slots, *args)


def body(
    tokens, timesteps, time_table, w_qkv, b_qv, w_out, b_out, w_in, b_in, w_back, b_back,
    gain_one, shift_one, gain_two, shift_two, cotangent,
):
    sentences = timesteps.shape[0]
    rows, dim = tokens.shape
    hc = w_out.shape[0]
    hid = w_back.shape[0]
    table_cols = time_table.shape[1]
    n_tensor = dim // hc
    me = lax.axis_index("tensor")
    part = lax.axis_index("dp")
    dp = lax.axis_size("dp")
    order = [me ^ k for k in range(n_tensor)]
    fast = dp == 8 and n_tensor == 4
    sds = jax.ShapeDtypeStruct
    nb = rows // BR
    unit = 1e9

    att_own = jnp.concatenate(
        [jnp.transpose(w_qkv, (1, 2, 0)).reshape(3 * hc, dim), w_out], axis=0
    )
    n_att = att_own.shape[0] // dp
    att_piece = lax.dynamic_slice_in_dim(att_own, part * n_att, n_att, 0)

    steps_iota = lax.broadcasted_iota(jnp.int32, (sentences, time_table.shape[0]), 1)
    picked = timesteps[:, None] == steps_iota
    own_rows = jnp.dot(picked.astype(BF16), time_table, preferred_element_type=F32)
    bias_count = 2 + hid // hc
    own_bias = jnp.concatenate([b_qv, b_in.reshape(-1, hc)])
    if fast:
        core = (part % 2).astype(jnp.int32).reshape(1)
        planes = jnp.pad(three(own_bias), ((0, sentences - 3 * bias_count), (0, 0)))
        note = jnp.concatenate(
            [own_rows.astype(BF16), jnp.zeros((sentences, 256 - hc), BF16), planes,
             jnp.zeros((sentences, dim - 256 - hc), BF16)], axis=1
        )
        message = jnp.concatenate([att_piece, note])
        got = [lax.ppermute(message, "tensor", flipped(4, k)) for k in (1, 2, 3)]
        mine_a = spread_plane([got[0][:n_att]])
        mine_b = spread_plane([got[1][:n_att], got[2][:n_att]])
        other_a = lax.ppermute(mine_a, "dp", flipped(8, 1))
        time_slots = jnp.stack([own_rows] + [m[n_att:, :hc].astype(F32) for m in got])
        bias_slots = jnp.stack(
            [own_bias] + [of_three(m[n_att:, 256 : 256 + hc], bias_count) for m in got]
        )
    else:
        core = jnp.zeros((1,), jnp.int32)
        (mine_a, mine_b), (other_a, other_b) = spread_any(att_piece, order, dp)
        time_slots = picked_rows(lax.all_gather(own_rows, "tensor", axis=0), order)
        bias_slots = picked_rows(lax.all_gather(own_bias, "tensor", axis=0), order)

    n_mlp = (dim + hid) // dp
    if fast:
        first = dim // n_mlp
        up = lax.dynamic_slice_in_dim(w_in, jnp.minimum(part, first - 1) * n_mlp, n_mlp, 0)
        down = lax.dynamic_slice_in_dim(w_back, jnp.maximum(part - first, 0) * n_mlp, n_mlp, 0)
        mlp_piece = jnp.where(part < first, up, down)
    else:
        mlp_piece = lax.dynamic_slice_in_dim(
            jnp.concatenate([w_in, w_back]), part * n_mlp, n_mlp, 0
        )
    mlp_all = lax.all_gather(mlp_piece, ("tensor", "dp"), axis=0, tiled=True)
    mlp_all = mlp_all.reshape(n_tensor, dim + hid, dim)

    time_rows = jnp.concatenate([time_slots[k] for k in range(n_tensor)], axis=1)
    for bit in range(n_tensor.bit_length() - 1):
        step = hc << bit
        swapped = jnp.concatenate(
            [time_rows[:, (j ^ 1) * step : ((j ^ 1) + 1) * step] for j in range(dim // step)],
            axis=1,
        )
        time_rows = jnp.where((me >> bit) % 2 == 1, swapped, time_rows)
    time_rows = time_rows.reshape(nb, BR // LEN, dim)
    bq, bv = bias_slots[:, 0].reshape(2, -1), bias_slots[:, 1].reshape(2, -1)
    bias_rows = jnp.concatenate([bq, jnp.zeros_like(bq), bv], axis=1)
    bi_rest = bias_slots[1:, 2:].reshape(3, hid)
    zero = jnp.zeros_like(b_out)
    vecs = jnp.stack([gain_one, shift_one, gain_two, shift_two, b_out, b_back, b_in, zero])

    grid = (nb,)
    width = 2 * hc
    time_spec = pl.BlockSpec((1, BR // LEN, dim), lambda i, *_: (i, 0, 0))
    vec = whole_spec((8, dim))
    own_spec = whole_spec((4 * hc, dim))
    piece_spec = lambda k: whole_spec((4, k, hc // 2, dim))
    bias_spec = whole_spec((2, 3 * width))
    weights = [pltpu.VMEM((3 * width, dim), BF16), pltpu.VMEM((width, dim), BF16)]
    back = [pltpu.VMEM((BR, 3 * width), BF16), pltpu.VMEM((BR, width), BF16)]

    n_one, qkv_a, p_a, mix_a, attn_part = call(
        attend_first, grid,
        [rows_spec(dim), time_spec, vec, own_spec, piece_spec(1), piece_spec(1), bias_spec],
        [rows_spec(dim), rows_spec(3 * width), rows_spec(width), rows_spec(width),
         rows_spec(dim)],
        [sds((rows, dim), BF16), sds((rows, 3 * width), BF16), sds((rows, width), BF16),
         sds((rows, width), BF16), sds((rows, dim), BF16)],
        weights, core,
        (tokens, time_rows, vecs, att_own, mine_a, other_a, bias_rows), 14 * unit,
    )
    if fast:
        mine_b, n_one = lax.optimization_barrier((mine_b, n_one))
        other_b = lax.ppermute(mine_b, "dp", flipped(8, 1))
    qkv_b, p_b, middle, n_two = call(
        attend_last, grid,
        [rows_spec(dim), time_spec, rows_spec(dim), rows_spec(dim), vec, piece_spec(2),
         piece_spec(2), bias_spec],
        [rows_spec(3 * width), rows_spec(width), rows_spec(dim), rows_spec(dim)],
        [sds((rows, 3 * width), BF16), sds((rows, width), BF16), sds((rows, dim), F32),
         sds((rows, dim), BF16)],
        weights + [pltpu.VMEM((BR, width), BF16)], core,
        (tokens, time_rows, n_one, attn_part, vecs, mine_b, other_b, bias_rows), 15 * unit,
    )
    out_acc, dn2_acc, mlp_grads, gbin = call(
        mlp_own, grid,
        [rows_spec(dim), rows_spec(dim), whole_spec((dim, hid)), whole_spec((hid, dim)), vec],
        [rows_spec(dim), rows_spec(dim), whole_spec((dim, 2 * hid)), whole_spec((1, hid))],
        [sds((rows, dim), BF16), sds((rows, dim), BF16), sds((dim, 2 * hid), BF16),
         sds((1, hid), F32)],
        [pltpu.VMEM((dim, 2 * hid), F32), pltpu.VMEM((8, hid), F32)], None,
        (n_two, cotangent, w_in, w_back, vecs), 21 * unit,
    )

    def scattered(grad):
        return lax.psum_scatter(grad, "dp", scatter_dimension=0, tiled=True)

    mlp_grads, mlp_all = lax.optimization_barrier((mlp_grads, mlp_all))
    mlp_grads = scattered(mlp_grads)
    mlp_spec = lambda k: slot_spec((dim + hid, dim), k)
    places = jnp.concatenate([me ^ jnp.arange(n_tensor, dtype=jnp.int32), core])
    spread_steps = jnp.pad(timesteps.astype(F32), (256, dim - 256 - sentences)).reshape(1, dim)
    output, d_mid, dn1_acc, att_grads, more = call(
        rest_and_back, grid,
        [rows_spec(dim), rows_spec(dim), rows_spec(dim), rows_spec(dim), rows_spec(dim), vec,
         mlp_spec(1), mlp_spec(2), mlp_spec(3), whole_spec((3, hid)),
         rows_spec(dim), rows_spec(width), rows_spec(3 * width), rows_spec(width), own_spec,
         piece_spec(1), piece_spec(1), whole_spec((1, dim)), whole_spec((1, dim))],
        [rows_spec(dim), rows_spec(dim), rows_spec(dim), whole_spec((dim, 4 * hc)), vec],
        [sds((rows, dim), BF16)] * 3 + [sds((dim, 4 * hc), BF16), sds((8, dim), F32)],
        [pltpu.VMEM((32, dim), F32)] + weights + back
        + [pltpu.VMEM((dim, 1024), F32), pltpu.VMEM((8, 3 * width), F32)],
        places,
        (n_two, cotangent, middle, out_acc, dn2_acc, vecs, mlp_all, mlp_all, mlp_all, bi_rest,
         n_one, mix_a, qkv_a, p_a, att_own, mine_a, other_a, gbin, spread_steps),
        62 * unit,
    )
    copies = dp if fast else 1
    if fast:
        parts = lax.all_to_all(
            att_grads.reshape(dp, dim // dp, 4 * hc), "dp", 0, 0, tiled=True
        )
    else:
        att_grads = scattered(att_grads).astype(F32)
    grad_tokens, terms, grad_win, grad_wback = call(
        back_last, grid,
        [rows_spec(dim), time_spec, rows_spec(dim), rows_spec(dim), vec,
         rows_spec(3 * width), rows_spec(width), piece_spec(2), piece_spec(2), vec,
         whole_spec(mlp_grads.shape)],
        [rows_spec(dim), whole_spec((copies, 16, dim)),
         whole_spec((dim // dp, hid)), whole_spec((dim // dp, hid))],
        [sds((rows, dim), BF16), sds((copies, 16, dim), F32),
         sds((dim // dp, hid), F32), sds((dim // dp, hid), F32)],
        weights + back + [pltpu.VMEM((16, dim), F32), pltpu.VMEM((sentences, dim), F32)],
        places,
        (tokens, time_rows, d_mid, dn1_acc, vecs, qkv_b, p_b, mine_b, other_b, more, mlp_grads),
        20 * unit,
    )

    if fast:
        terms, parts = lax.optimization_barrier((terms, parts))
        terms = lax.all_to_all(terms, "dp", 0, 0, tiled=True)
    else:
        terms = lax.all_gather(terms, "dp", axis=0, tiled=True)
    if fast:
        att_grads = jnp.sum(parts.astype(F32), axis=0)
    grad_wqkv = att_grads[:, : 3 * hc].reshape(-1, 3, hc)
    grad_wout = att_grads[:, 3 * hc :].T
    all_cols = terms[:, :8].reshape(-1, table_cols)
    small = jnp.sum(terms[:, 8:], axis=0)
    all_steps = terms[:, -1, 256 : 256 + sentences].astype(jnp.int32)
    all_steps = jnp.transpose(all_steps.reshape(dp, 4, 8), (0, 2, 1)).reshape(-1)
    all_picked = all_steps[:, None] == lax.broadcasted_iota(
        jnp.int32, (all_steps.shape[0], time_table.shape[0]), 1
    )
    grad_table = lax.dot_general(
        all_picked.astype(F32), all_cols, (((0,), (0,)), ((), ())),
        precision=HIGHEST_PREC, preferred_element_type=F32,
    )
    grad_bqv = jnp.stack([small[7, :hc], small[7, dim - 256 : dim - 256 + hc]])
    return (
        output, grad_tokens, grad_table, grad_wqkv, grad_bqv, grad_wout, small[2], grad_win,
        small[6], grad_wback.T, small[3], small[4], small[5], small[0], small[1],
    )


def picked_rows(array, order):
    return jnp.concatenate([lax.dynamic_slice_in_dim(array, k, 1, 0) for k in order])


def three(value):
    parts = []
    for _ in range(3):
        low = lax.reduce_precision(value, 8, 7)
        parts.append(low.astype(BF16))
        value = value - low
    return jnp.concatenate(parts)


def of_three(rows, n):
    rows = rows.astype(F32)
    return (rows[2 * n : 3 * n] + rows[n : 2 * n]) + rows[:n]


def flipped(n, bits):
    return [(i, i ^ bits) for i in range(n)]


def spread_plane(slots):
    slots = jnp.stack(slots)
    whole = jnp.broadcast_to(slots[None], (4,) + slots.shape)
    return lax.all_to_all(
        whole, "dp", 0, 0, tiled=True, axis_index_groups=[[0, 2, 4, 6], [1, 3, 5, 7]]
    )


def spread_any(piece, order, dp):
    shards = lax.all_gather(piece, ("tensor", "dp"), axis=0, tiled=True)
    n_tensor = len(order)
    rows = piece.shape[0] * dp
    shards = picked_rows(shards.reshape(n_tensor, rows, -1), order[1:])
    shards = shards.reshape(n_tensor - 1, 4, 2, rows // 8, -1)
    halves = [jnp.transpose(shards[:, :, c], (1, 0, 2, 3)) for c in (0, 1)]
    return tuple((h[:, :1], h[:, 1:]) for h in halves)


def solution(mesh):
    return jax.shard_map(
        body,
        mesh=mesh,
        in_specs=(
            P("dp", None), P("dp"), P(None, "tensor"), P(None, None, "tensor"), P(None, "tensor"),
            P("tensor", None), P(), P(None, "tensor"), P("tensor"), P("tensor", None), P(), P(),
            P(), P(), P(), P("dp", None),
        ),
        out_specs=(
            P("dp", None), P("dp", None), P(None, "tensor"), P("dp", None, "tensor"),
            P(None, "tensor"), P("tensor", "dp"), P(), P("dp", "tensor"), P("tensor"),
            P("tensor", "dp"), P(), P(), P(), P(), P(),
        ),
        check_vma=False,
    )
```

```python
import functools

import jax
import jax.numpy as jnp
from jax import lax
from jax.experimental import pallas as pl
from jax.experimental.pallas import tpu as pltpu
from jax.sharding import PartitionSpec as P

HEAD = 64
HEADS = 3
LEN = 64
EPS = 1e-05
BR = 512
VMEM_BYTES = 58 * 1024 * 1024
HIGHEST_PREC = lax.Precision.HIGHEST
F32 = jnp.float32
BF16 = jnp.bfloat16


def dot_nn(a, b):
    return lax.dot_general(a, b, (((1,), (0,)), ((), ())), preferred_element_type=F32)


def dot_nt(a, b):
    return lax.dot_general(a, b, (((1,), (1,)), ((), ())), preferred_element_type=F32)


def dot_tn(a, b):
    return lax.dot_general(a, b, (((0,), (0,)), ((), ())), preferred_element_type=F32)


def cost(out_shape, args, flops):
    size = sum(v.size * v.dtype.itemsize for v in (*args, *out_shape))
    return pl.CostEstimate(flops=int(flops), bytes_accessed=int(size), transcendentals=0)


def params():
    return pltpu.CompilerParams(
        dimension_semantics=("arbitrary",), vmem_limit_bytes=VMEM_BYTES
    )


def rows_spec(width, rows=BR):
    return pl.BlockSpec((rows, width), lambda i, *_: (i, 0))


def whole_spec(shape):
    return pl.BlockSpec(shape, lambda i, *_: (0,) * len(shape), pipeline_mode=pl.Buffered(1))


def slot_spec(shape, k):
    return pl.BlockSpec(
        (1,) + shape, lambda i, s: (s[k],) + (0,) * len(shape), pipeline_mode=pl.Buffered(1)
    )


def normed(x):
    mean = jnp.mean(x, axis=-1, keepdims=True)
    centred = x - mean
    spread = jnp.mean(centred * centred, axis=-1, keepdims=True)
    inv = lax.rsqrt(spread + EPS)
    return centred * inv, inv


def norm_back(d_out, gain, xhat, inv):
    gy = d_out * gain
    m1 = jnp.mean(gy, axis=-1, keepdims=True)
    m2 = jnp.mean(gy * xhat, axis=-1, keepdims=True)
    return inv * (gy - m1 - xhat * m2)


def fold8(x):
    return jnp.sum(x.reshape(x.shape[0] // 8, 8, x.shape[1]), axis=0)


def entry_of(tok_ref, time_ref):
    tok = tok_ref[...].astype(F32)
    n = tok.shape[0] // LEN
    return (tok.reshape(n, LEN, tok.shape[1]) + time_ref[0][:, None, :]).reshape(tok.shape)


def half_masks():
    lane = lax.broadcasted_iota(jnp.int32, (LEN, 2 * HEAD), 1)
    low = (lane < HEAD).astype(F32)
    return low.astype(BF16), (1.0 - low).astype(BF16), lane < HEAD


def block_diag(x, mlo, mhi):
    return jnp.concatenate([x * mlo, x * mhi], axis=0)


def load_own(att, wqkv, wo, s):
    hc = HEADS * HEAD
    for t in range(3):
        wqkv[(2 * t + s) * hc : (2 * t + s + 1) * hc, :] = att[t * hc : (t + 1) * hc, :]
    wo[s * hc : (s + 1) * hc, :] = att[3 * hc :, :]


def load_pieces(core, mine, other, k, wqkv, wo, s):
    hc = HEADS * HEAD
    n = hc // 2
    for src, at in ((mine, core * n), (other, (1 - core) * n)):
        for t in range(3):
            wqkv[pl.ds(pl.multiple_of((2 * t + s) * hc + at, 16), n), :] = src[t, k]
        wo[pl.ds(pl.multiple_of(s * hc + at, 16), n), :] = src[3, k]


def tile_list(rows, width):
    return [(s, j) for s in range(rows // LEN) for j in range(width // 128)]


def tile(ref, st, part=0, width=0):
    s, j = st
    return ref[s * LEN : (s + 1) * LEN, part * width + j * 128 : part * width + (j + 1) * 128]


def put_tile(ref, st, value, part=0, width=0):
    s, j = st
    ref[s * LEN : (s + 1) * LEN, part * width + j * 128 : part * width + (j + 1) * 128] = (
        value.astype(BF16)
    )


def attend(n_one, wqkv, wo, bias, qkv_ref, p_ref, mix_ref):
    width = wo.shape[0]
    qkv_ref[...] = (dot_nt(n_one, wqkv[...]) + bias).astype(BF16)
    mlo, mhi, low = half_masks()
    tiles = tile_list(n_one.shape[0], width)
    scores = [
        dot_nt(tile(qkv_ref, t, 1, width), block_diag(tile(qkv_ref, t, 0, width), mlo, mhi))
        for t in tiles
    ]
    probs = []
    for t, sc in zip(tiles, scores):
        top = jnp.max(sc, axis=0, keepdims=True)
        e = jnp.exp((sc - top) * (HEAD**-0.5))
        p = (e * (1.0 / jnp.sum(e, axis=0, keepdims=True))).astype(BF16)
        probs.append(p)
        put_tile(p_ref, t, p)
    both = [dot_tn(p, tile(qkv_ref, t, 2, width)) for t, p in zip(tiles, probs)]
    for t, r in zip(tiles, both):
        put_tile(mix_ref, t, jnp.where(low, r[:LEN], r[LEN:]))
    return dot_nn(mix_ref[...], wo[...])


def attend_first(
    core, tok, time, vecs, own, mine, other, bias,
    n_one_ref, qkv_ref, p_ref, mix_ref, part_ref, wqkv, wo,
):
    @pl.when(pl.program_id(0) == 0)
    def _():
        load_own(own, wqkv, wo, 0)
        load_pieces(core[0], mine, other, 0, wqkv, wo, 1)

    xhat, _ = normed(entry_of(tok, time))
    n_one = (xhat * vecs[0:1, :] + vecs[1:2, :]).astype(BF16)
    n_one_ref[...] = n_one
    part = attend(n_one, wqkv, wo, bias[0:1, :], qkv_ref, p_ref, mix_ref)
    part_ref[...] = part.astype(part_ref.dtype)


def attend_last(
    core, tok, time, n_one, part, vecs, mine, other, bias,
    qkv_ref, p_ref, middle_ref, n_two_ref, wqkv, wo, mix_ref,
):
    @pl.when(pl.program_id(0) == 0)
    def _():
        load_pieces(core[0], mine, other, 0, wqkv, wo, 0)
        load_pieces(core[0], mine, other, 1, wqkv, wo, 1)

    more = attend(n_one[...], wqkv, wo, bias[1:2, :], qkv_ref, p_ref, mix_ref)
    middle = entry_of(tok, time) + part[...].astype(F32) + more + vecs[4:5, :]
    middle_ref[...] = middle
    xhat, _ = normed(middle)
    n_two_ref[...] = (xhat * vecs[2:3, :] + vecs[3:4, :]).astype(BF16)


ERF_P = 0.3275911
ERF_A = (0.254829592, -0.284496736, 1.421413741, -1.453152027, 1.061405429)


def gelu_both(x):
    bell = jnp.exp(x * x * (-0.5))
    t = 1.0 / (1.0 + jnp.abs(x) * (ERF_P * 0.5**0.5))
    poly = t * (
        0.5 * ERF_A[0]
        + t * (0.5 * ERF_A[1] + t * (0.5 * ERF_A[2] + t * (0.5 * ERF_A[3] + t * (0.5 * ERF_A[4]))))
    )
    tail = poly * bell
    cdf = jnp.where(x >= 0, 1.0 - tail, tail)
    return x * cdf, cdf + x * bell * 0.3989422804014327


def mlp_slot(n_two, c, wi, wb, b):
    pre = dot_nn(n_two, wi) + b
    d_act = dot_nt(c, wb)
    act, slope = gelu_both(pre)
    act = act.astype(BF16)
    d_pre = (d_act * slope).astype(BF16)
    return act, d_pre


def mlp_own(n_two, c, wi, wb, vecs, out_ref, dn2_ref, grad_ref, gbin_ref, acc, sums):
    hid = wb.shape[0]

    @pl.when(pl.program_id(0) == 0)
    def _():
        acc[...] = jnp.zeros_like(acc)
        sums[...] = jnp.zeros_like(sums)

    act, d_pre = mlp_slot(n_two[...], c[...], wi[...], wb[...], vecs[6:7, :])
    sums[...] += fold8(d_pre.astype(F32))
    out_ref[...] = dot_nn(act, wb[...]).astype(BF16)
    dn2_ref[...] = dot_nt(d_pre, wi[...]).astype(BF16)
    acc[:, :hid] += dot_tn(n_two[...], d_pre)
    acc[:, hid:] += dot_tn(c[...], act)

    @pl.when(pl.program_id(0) == pl.num_programs(0) - 1)
    def _():
        grad_ref[...] = acc[...].astype(BF16)
        gbin_ref[...] = jnp.sum(sums[...], axis=0, keepdims=True)


def total(rows):
    return jnp.sum(rows, axis=0, keepdims=True)


def start_sums(sums):
    @pl.when(pl.program_id(0) == 0)
    def _():
        sums[...] = jnp.zeros_like(sums)


def add_sums(sums, terms):
    for k, term in enumerate(terms):
        sums[8 * k : 8 * k + 8, :] += fold8(term)


def end_sums(sums, sums_ref):
    @pl.when(pl.program_id(0) == pl.num_programs(0) - 1)
    def _():
        for k in range(sums_ref.shape[0]):
            sums_ref[k : k + 1, :] = jnp.sum(sums[8 * k : 8 * k + 8, :], axis=0, keepdims=True)


def attend_back(dml, qkv, p, wqkv, wo, dqkv, dmix):
    width = wo.shape[0]
    scale = HEAD**-0.5
    dmix[...] = dot_nt(dml, wo[...]).astype(BF16)
    mlo, mhi, low = half_masks()
    tiles = tile_list(dml.shape[0], width)
    d_outs = [block_diag(tile(dmix, t), mlo, mhi) for t in tiles]
    d_ps = [dot_nt(tile(qkv, t, 2, width), d) for t, d in zip(tiles, d_outs)]
    for t, d in zip(tiles, d_outs):
        put_tile(dqkv, t, dot_nn(tile(p, t), d), 2, width)
    d_ss = []
    for t, d_p in zip(tiles, d_ps):
        pf = tile(p, t).astype(F32)
        g = pf * d_p
        d_ss.append((g - pf * jnp.sum(g, axis=0, keepdims=True)).astype(BF16))
    for t, d_s in zip(tiles, d_ss):
        put_tile(
            dqkv, t, dot_nn(d_s, block_diag(tile(qkv, t, 0, width), mlo, mhi)) * scale, 1, width
        )
    both = [dot_tn(d_s, tile(qkv, t, 1, width)) for t, d_s in zip(tiles, d_ss)]
    for t, r in zip(tiles, both):
        put_tile(dqkv, t, jnp.where(low, r[:LEN], r[LEN:]) * scale)
    return dot_nn(dqkv[...], wqkv[...])


def rest_and_back(
    slots, n_two, c, middle, out_in, dn2_in, vecs, w1, w2, w3, b,
    n_one, mix, qkv, p, own, mine, other, gbin, steps,
    out_ref, dmid_ref, dn1_ref, grad_ref, more_ref,
    sums, wqkv, wo, dqkv, dmix, acc, bias_sums,
):
    @pl.when(pl.program_id(0) == 0)
    def _():
        load_own(own, wqkv, wo, 0)
        load_pieces(slots[4], mine, other, 0, wqkv, wo, 1)
        acc[...] = jnp.zeros_like(acc)

    start_sums(sums)
    start_sums(bias_sums)

    dim = n_two.shape[1]
    out = out_in[...].astype(F32)
    dn2 = dn2_in[...].astype(F32)
    for k, w in enumerate((w1, w2, w3)):
        wi = w[:4, 0].reshape(-1, dim)
        wb = w[4:, 0].reshape(-1, dim)
        act, d_pre = mlp_slot(n_two[...], c[...], wi, wb, b[k : k + 1, :])
        out = out + dot_nn(act, wb)
        dn2 = dn2 + dot_nt(d_pre, wi)
    mid = middle[...]
    cot = c[...].astype(F32)
    out_ref[...] = (mid + out + vecs[5:6, :]).astype(BF16)
    xhat, inv = normed(mid)
    d_mid = cot + norm_back(dn2, vecs[2:3, :], xhat, inv)
    add_sums(sums, (dn2 * xhat, dn2, d_mid, cot))

    dml = d_mid.astype(BF16)
    dmid_ref[...] = dml
    dn1_ref[...] = attend_back(dml, qkv, p, wqkv, wo, dqkv, dmix).astype(dn1_ref.dtype)
    width = wo.shape[0]
    for t in range(3):
        acc[:, t * 256 : (t + 1) * 256] += dot_tn(
            n_one[...], dqkv[:, t * width : t * width + 256]
        )
    acc[:, 768:] += dot_tn(dml, mix[:, :256])
    add_sums(bias_sums, (dqkv[...].astype(F32),))

    @pl.when(pl.program_id(0) == pl.num_programs(0) - 1)
    def _():
        for r in range(4):
            more_ref[r : r + 1, :] = total(sums[8 * r : 8 * r + 8, :])
        more_ref[4:6, :] = jnp.zeros_like(more_ref[4:6, :])
        more_ref[6:7, :] = gbin[...]
        more_ref[7:8, :] = steps[...]
        bias = total(bias_sums[...])
        more_ref[7:8, :256] = bias[:, :256]
        more_ref[7:8, 512:] = bias[:, 2 * width : 2 * width + 256]
        hc = HEADS * HEAD
        for t in range(4):
            grad_ref[:, t * hc : (t + 1) * hc] = acc[:, t * 256 : t * 256 + hc].astype(BF16)


def back_last(
    places, tok, time, dmid, dn1, vecs, qkv, p, mine, other, more, mlp_sums,
    gtok_ref, terms_ref, gwin_ref, gwback_ref, wqkv, wo, dqkv, dmix, sums, per,
):
    @pl.when(pl.program_id(0) == 0)
    def _():
        load_pieces(places[4], mine, other, 0, wqkv, wo, 0)
        load_pieces(places[4], mine, other, 1, wqkv, wo, 1)
        hid = gwin_ref.shape[1]
        gwin_ref[...] = mlp_sums[:, :hid].astype(F32)
        gwback_ref[...] = mlp_sums[:, hid:].astype(F32)

    start_sums(sums)
    d_n = dn1[...].astype(F32) + attend_back(dmid[...], qkv, p, wqkv, wo, dqkv, dmix)
    xhat, inv = normed(entry_of(tok, time))
    d_entry = dmid[...].astype(F32) + norm_back(d_n, vecs[0:1, :], xhat, inv)
    gtok_ref[...] = d_entry.astype(BF16)
    n = d_entry.shape[0] // LEN
    at = pl.multiple_of(pl.program_id(0) * n, 8)
    per[pl.ds(at, n), :] = jnp.sum(d_entry.reshape(n, LEN, -1), axis=1)
    add_sums(sums, (d_n * xhat, d_n))

    @pl.when(pl.program_id(0) == pl.num_programs(0) - 1)
    def _():
        cols = per.shape[1] // 4
        own = per[:, :cols]
        for j in range(1, 4):
            own = jnp.where(places[0] == j, per[:, j * cols : (j + 1) * cols], own)
        for j in range(4):
            terms_ref[0, :8, j * cols : (j + 1) * cols] = own[8 * j : 8 * j + 8, :]
        terms_ref[0, 8:12, :] = more[0:4, :]
        terms_ref[0, 12:13, :] = total(sums[0:8, :])
        terms_ref[0, 13:14, :] = total(sums[8:16, :])
        terms_ref[0, 14:16, :] = more[6:8, :]
        for k in range(1, terms_ref.shape[0]):
            terms_ref[k] = terms_ref[0]


def call(kernel, grid, in_specs, out_specs, out_shape, scratch, slots, args, flops):
    if slots is None:
        return pl.pallas_call(
            kernel, grid=grid, in_specs=in_specs, out_specs=out_specs, out_shape=out_shape,
            scratch_shapes=scratch, compiler_params=params(),
            cost_estimate=cost(out_shape, args, flops),
        )(*args)
    return pl.pallas_call(
        kernel,
        grid_spec=pltpu.PrefetchScalarGridSpec(
            num_scalar_prefetch=1, grid=grid, in_specs=in_specs, out_specs=out_specs,
            scratch_shapes=scratch,
        ),
        out_shape=out_shape,
        compiler_params=params(),
        cost_estimate=cost(out_shape, args, flops),
    )(slots, *args)


def body(
    tokens, timesteps, time_table, w_qkv, b_qv, w_out, b_out, w_in, b_in, w_back, b_back,
    gain_one, shift_one, gain_two, shift_two, cotangent,
):
    sentences = timesteps.shape[0]
    rows, dim = tokens.shape
    hc = w_out.shape[0]
    hid = w_back.shape[0]
    table_cols = time_table.shape[1]
    n_tensor = dim // hc
    me = lax.axis_index("tensor")
    part = lax.axis_index("dp")
    dp = lax.axis_size("dp")
    order = [me ^ k for k in range(n_tensor)]
    fast = dp == 8 and n_tensor == 4
    sds = jax.ShapeDtypeStruct
    nb = rows // BR
    unit = 1e9

    att_own = jnp.concatenate(
        [jnp.transpose(w_qkv, (1, 2, 0)).reshape(3 * hc, dim), w_out], axis=0
    )
    n_att = att_own.shape[0] // dp
    att_piece = lax.dynamic_slice_in_dim(att_own, part * n_att, n_att, 0)

    steps_iota = lax.broadcasted_iota(jnp.int32, (sentences, time_table.shape[0]), 1)
    picked = timesteps[:, None] == steps_iota
    own_rows = jnp.dot(picked.astype(BF16), time_table, preferred_element_type=F32)
    bias_count = 2 + hid // hc
    own_bias = jnp.concatenate([b_qv, b_in.reshape(-1, hc)])
    if fast:
        core = (part % 2).astype(jnp.int32).reshape(1)
        planes = jnp.pad(three(own_bias), ((0, sentences - 3 * bias_count), (0, 0)))
        note = jnp.concatenate(
            [own_rows.astype(BF16), jnp.zeros((sentences, 256 - hc), BF16), planes,
             jnp.zeros((sentences, dim - 256 - hc), BF16)], axis=1
        )
        message = jnp.concatenate([att_piece, note])
        got = [lax.ppermute(message, "tensor", flipped(4, k)) for k in (1, 2, 3)]
        mine_a = spread_plane([got[0][:n_att]])
        mine_b = spread_plane([got[1][:n_att], got[2][:n_att]])
        other_a = lax.ppermute(mine_a, "dp", flipped(8, 1))
        time_slots = jnp.stack([own_rows] + [m[n_att:, :hc].astype(F32) for m in got])
        bias_slots = jnp.stack(
            [own_bias] + [of_three(m[n_att:, 256 : 256 + hc], bias_count) for m in got]
        )
    else:
        core = jnp.zeros((1,), jnp.int32)
        (mine_a, mine_b), (other_a, other_b) = spread_any(att_piece, order, dp)
        time_slots = picked_rows(lax.all_gather(own_rows, "tensor", axis=0), order)
        bias_slots = picked_rows(lax.all_gather(own_bias, "tensor", axis=0), order)

    n_mlp = (dim + hid) // dp
    if fast:
        first = dim // n_mlp
        up = lax.dynamic_slice_in_dim(w_in, jnp.minimum(part, first - 1) * n_mlp, n_mlp, 0)
        down = lax.dynamic_slice_in_dim(w_back, jnp.maximum(part - first, 0) * n_mlp, n_mlp, 0)
        mlp_piece = jnp.where(part < first, up, down)
    else:
        mlp_piece = lax.dynamic_slice_in_dim(
            jnp.concatenate([w_in, w_back]), part * n_mlp, n_mlp, 0
        )
    mlp_all = lax.all_gather(mlp_piece, ("dp", "tensor"), axis=0, tiled=True)
    mlp_all = mlp_all.reshape(dp, n_tensor, n_mlp, dim)
    if not fast:
        mlp_all = jnp.transpose(mlp_all, (0, 2, 1, 3)).reshape(8, -1, n_tensor, dim)
        mlp_all = jnp.transpose(mlp_all, (0, 2, 1, 3))

    time_rows = jnp.concatenate([time_slots[k] for k in range(n_tensor)], axis=1)
    for bit in range(n_tensor.bit_length() - 1):
        step = hc << bit
        swapped = jnp.concatenate(
            [time_rows[:, (j ^ 1) * step : ((j ^ 1) + 1) * step] for j in range(dim // step)],
            axis=1,
        )
        time_rows = jnp.where((me >> bit) % 2 == 1, swapped, time_rows)
    time_rows = time_rows.reshape(nb, BR // LEN, dim)
    bq, bv = bias_slots[:, 0].reshape(2, -1), bias_slots[:, 1].reshape(2, -1)
    bias_rows = jnp.concatenate([bq, jnp.zeros_like(bq), bv], axis=1)
    bi_rest = bias_slots[1:, 2:].reshape(3, hid)
    zero = jnp.zeros_like(b_out)
    vecs = jnp.stack([gain_one, shift_one, gain_two, shift_two, b_out, b_back, b_in, zero])

    grid = (nb,)
    width = 2 * hc
    time_spec = pl.BlockSpec((1, BR // LEN, dim), lambda i, *_: (i, 0, 0))
    vec = whole_spec((8, dim))
    own_spec = whole_spec((4 * hc, dim))
    piece_spec = lambda k: whole_spec((4, k, hc // 2, dim))
    bias_spec = whole_spec((2, 3 * width))
    weights = [pltpu.VMEM((3 * width, dim), BF16), pltpu.VMEM((width, dim), BF16)]
    back = [pltpu.VMEM((BR, 3 * width), BF16), pltpu.VMEM((BR, width), BF16)]

    n_one, qkv_a, p_a, mix_a, attn_part = call(
        attend_first, grid,
        [rows_spec(dim), time_spec, vec, own_spec, piece_spec(1), piece_spec(1), bias_spec],
        [rows_spec(dim), rows_spec(3 * width), rows_spec(width), rows_spec(width),
         rows_spec(dim)],
        [sds((rows, dim), BF16), sds((rows, 3 * width), BF16), sds((rows, width), BF16),
         sds((rows, width), BF16), sds((rows, dim), BF16)],
        weights, core,
        (tokens, time_rows, vecs, att_own, mine_a, other_a, bias_rows), 14 * unit,
    )
    if fast:
        mine_b, n_one = lax.optimization_barrier((mine_b, n_one))
        other_b = lax.ppermute(mine_b, "dp", flipped(8, 1))
    qkv_b, p_b, middle, n_two = call(
        attend_last, grid,
        [rows_spec(dim), time_spec, rows_spec(dim), rows_spec(dim), vec, piece_spec(2),
         piece_spec(2), bias_spec],
        [rows_spec(3 * width), rows_spec(width), rows_spec(dim), rows_spec(dim)],
        [sds((rows, 3 * width), BF16), sds((rows, width), BF16), sds((rows, dim), F32),
         sds((rows, dim), BF16)],
        weights + [pltpu.VMEM((BR, width), BF16)], core,
        (tokens, time_rows, n_one, attn_part, vecs, mine_b, other_b, bias_rows), 15 * unit,
    )
    out_acc, dn2_acc, mlp_grads, gbin = call(
        mlp_own, grid,
        [rows_spec(dim), rows_spec(dim), whole_spec((dim, hid)), whole_spec((hid, dim)), vec],
        [rows_spec(dim), rows_spec(dim), whole_spec((dim, 2 * hid)), whole_spec((1, hid))],
        [sds((rows, dim), BF16), sds((rows, dim), BF16), sds((dim, 2 * hid), BF16),
         sds((1, hid), F32)],
        [pltpu.VMEM((dim, 2 * hid), F32), pltpu.VMEM((8, hid), F32)], None,
        (n_two, cotangent, w_in, w_back, vecs), 21 * unit,
    )

    def scattered(grad):
        return lax.psum_scatter(grad, "dp", scatter_dimension=0, tiled=True)

    mlp_grads, mlp_all = lax.optimization_barrier((mlp_grads, mlp_all))
    mlp_grads = scattered(mlp_grads)
    mlp_spec = lambda k: pl.BlockSpec(
        (8, 1, (dim + hid) // 8, dim), lambda i, s: (0, s[k], 0, 0),
        pipeline_mode=pl.Buffered(1),
    )
    places = jnp.concatenate([me ^ jnp.arange(n_tensor, dtype=jnp.int32), core])
    spread_steps = jnp.pad(timesteps.astype(F32), (256, dim - 256 - sentences)).reshape(1, dim)
    output, d_mid, dn1_acc, att_grads, more = call(
        rest_and_back, grid,
        [rows_spec(dim), rows_spec(dim), rows_spec(dim), rows_spec(dim), rows_spec(dim), vec,
         mlp_spec(1), mlp_spec(2), mlp_spec(3), whole_spec((3, hid)),
         rows_spec(dim), rows_spec(width), rows_spec(3 * width), rows_spec(width), own_spec,
         piece_spec(1), piece_spec(1), whole_spec((1, dim)), whole_spec((1, dim))],
        [rows_spec(dim), rows_spec(dim), rows_spec(dim), whole_spec((dim, 4 * hc)), vec],
        [sds((rows, dim), BF16)] * 3 + [sds((dim, 4 * hc), BF16), sds((8, dim), F32)],
        [pltpu.VMEM((32, dim), F32)] + weights + back
        + [pltpu.VMEM((dim, 1024), F32), pltpu.VMEM((8, 3 * width), F32)],
        places,
        (n_two, cotangent, middle, out_acc, dn2_acc, vecs, mlp_all, mlp_all, mlp_all, bi_rest,
         n_one, mix_a, qkv_a, p_a, att_own, mine_a, other_a, gbin, spread_steps),
        62 * unit,
    )
    copies = dp if fast else 1
    if fast:
        parts = lax.all_to_all(
            att_grads.reshape(dp, dim // dp, 4 * hc), "dp", 0, 0, tiled=True
        )
    else:
        att_grads = scattered(att_grads).astype(F32)
    grad_tokens, terms, grad_win, grad_wback = call(
        back_last, grid,
        [rows_spec(dim), time_spec, rows_spec(dim), rows_spec(dim), vec,
         rows_spec(3 * width), rows_spec(width), piece_spec(2), piece_spec(2), vec,
         whole_spec(mlp_grads.shape)],
        [rows_spec(dim), whole_spec((copies, 16, dim)),
         whole_spec((dim // dp, hid)), whole_spec((dim // dp, hid))],
        [sds((rows, dim), BF16), sds((copies, 16, dim), F32),
         sds((dim // dp, hid), F32), sds((dim // dp, hid), F32)],
        weights + back + [pltpu.VMEM((16, dim), F32), pltpu.VMEM((sentences, dim), F32)],
        places,
        (tokens, time_rows, d_mid, dn1_acc, vecs, qkv_b, p_b, mine_b, other_b, more, mlp_grads),
        20 * unit,
    )

    if fast:
        terms, parts = lax.optimization_barrier((terms, parts))
        terms = lax.all_to_all(terms, "dp", 0, 0, tiled=True)
    else:
        terms = lax.all_gather(terms, "dp", axis=0, tiled=True)
    if fast:
        att_grads = jnp.sum(parts.astype(F32), axis=0)
    grad_wqkv = att_grads[:, : 3 * hc].reshape(-1, 3, hc)
    grad_wout = att_grads[:, 3 * hc :].T
    all_cols = terms[:, :8].reshape(-1, table_cols)
    small = jnp.sum(terms[:, 8:], axis=0)
    all_steps = terms[:, -1, 256 : 256 + sentences].astype(jnp.int32)
    all_steps = jnp.transpose(all_steps.reshape(dp, 4, 8), (0, 2, 1)).reshape(-1)
    all_picked = all_steps[:, None] == lax.broadcasted_iota(
        jnp.int32, (all_steps.shape[0], time_table.shape[0]), 1
    )
    grad_table = lax.dot_general(
        all_picked.astype(F32), all_cols, (((0,), (0,)), ((), ())),
        precision=HIGHEST_PREC, preferred_element_type=F32,
    )
    grad_bqv = jnp.stack([small[7, :hc], small[7, dim - 256 : dim - 256 + hc]])
    return (
        output, grad_tokens, grad_table, grad_wqkv, grad_bqv, grad_wout, small[2], grad_win,
        small[6], grad_wback.T, small[3], small[4], small[5], small[0], small[1],
    )


def picked_rows(array, order):
    return jnp.concatenate([lax.dynamic_slice_in_dim(array, k, 1, 0) for k in order])


def three(value):
    parts = []
    for _ in range(3):
        low = lax.reduce_precision(value, 8, 7)
        parts.append(low.astype(BF16))
        value = value - low
    return jnp.concatenate(parts)


def of_three(rows, n):
    rows = rows.astype(F32)
    return (rows[2 * n : 3 * n] + rows[n : 2 * n]) + rows[:n]


def flipped(n, bits):
    return [(i, i ^ bits) for i in range(n)]


def spread_plane(slots):
    slots = jnp.stack(slots)
    whole = jnp.broadcast_to(slots[None], (4,) + slots.shape)
    return lax.all_to_all(
        whole, "dp", 0, 0, tiled=True, axis_index_groups=[[0, 2, 4, 6], [1, 3, 5, 7]]
    )


def spread_any(piece, order, dp):
    shards = lax.all_gather(piece, ("tensor", "dp"), axis=0, tiled=True)
    n_tensor = len(order)
    rows = piece.shape[0] * dp
    shards = picked_rows(shards.reshape(n_tensor, rows, -1), order[1:])
    shards = shards.reshape(n_tensor - 1, 4, 2, rows // 8, -1)
    halves = [jnp.transpose(shards[:, :, c], (1, 0, 2, 3)) for c in (0, 1)]
    return tuple((h[:, :1], h[:, 1:]) for h in halves)


def solution(mesh):
    return jax.shard_map(
        body,
        mesh=mesh,
        in_specs=(
            P("dp", None), P("dp"), P(None, "tensor"), P(None, None, "tensor"), P(None, "tensor"),
            P("tensor", None), P(), P(None, "tensor"), P("tensor"), P("tensor", None), P(), P(),
            P(), P(), P(), P("dp", None),
        ),
        out_specs=(
            P("dp", None), P("dp", None), P(None, "tensor"), P("dp", None, "tensor"),
            P(None, "tensor"), P("tensor", "dp"), P(), P("dp", "tensor"), P("tensor"),
            P("tensor", "dp"), P(), P(), P(), P(), P(),
        ),
        check_vma=False,
    )
```
